128 devices in a mesh: grp: 32 (over x, y, z_lo), mem: 4 (over z_hi, core).
Axes of the slice: x: 4, y: 4, z: 4 (z_hi: 2, z_lo: 2; z = z_hi * 2 + z_lo), core: 2. Of those that a mesh axis runs over, the one named last changes fastest.
Arguments:
- points: float32 [11, 32768], P(None, ('grp', 'mem')), may hold values from -6 to 6
- inv_length: float32 [11], replicated, may hold values from 0.15 to 0.6
- out_scale: float32 [1], replicated, may hold values from 0.5 to 2
- noise: float32 [1], replicated, may hold values from 0.5 to 1.5
- solution: float32 [8, 32768], P(None, ('grp', 'mem')), may hold values from -6 to 6
- residual: float32 [8, 32768], P(None, ('grp', 'mem')), may hold values from -6 to 6
- direction: float32 [8, 32768], P(None, ('grp', 'mem')), may hold values from -6 to 6
Outputs:
- solution_out: float32 [8, 32768], P(None, ('grp', 'mem'))
- residual_out: float32 [8, 32768], P(None, ('grp', 'mem'))
- direction_out: float32 [8, 32768], P(None, ('grp', 'mem'))
The draws below stay inside these ranges and needn't reach their ends.
All inputs are finite; a program needn't handle non-finite values.
Results may differ from the reference program's by a relative error of at most 0.0003.
Values sent between devices are 32-bit elements; how exact they have to be, the bound alone decides.
A program may use at most 128 MiB of HBM per device.

```python
import math
import jax
import jax.numpy as jnp
from jax import lax

FEAT = 11
VEC = 8
ITERS = 2
NPTS = 32768


def levels(stream_key, dims, cuts, least, top_value):
    def one(axis_at, parts):
        draws = jax.random.uniform(jax.random.fold_in(jax.random.fold_in(stream_key, 6), axis_at), (parts,), jnp.float32, least / len(cuts), top_value / len(cuts))
        return jnp.repeat(jnp.exp(draws), dims[axis_at] // parts).reshape((-1,) + (1,) * (len(dims) - axis_at - 1))

    loudness = one(*cuts[0])
    for cut in cuts[1:]:
        loudness = loudness * one(*cut)
    return loudness


def bell_draw(own_key, dims, deviation, bound, cuts=(), kind=jnp.bfloat16):
    entries = deviation * jax.random.normal(own_key, dims, jnp.float32)
    if cuts:
        entries = entries * levels(own_key, dims, cuts, -0.22, 0.18)
    return jnp.clip(entries, -bound, bound).astype(kind)


def setup_inputs(seed: int = 0) -> dict:
    seeds = jax.random.split(jax.random.key(seed), 8)
    points = bell_draw(seeds[0], (FEAT, NPTS), 1.0, 6.0, ((1, 128),), jnp.float32)
    inv_length = jnp.clip(jnp.exp(jax.random.uniform(seeds[1], (FEAT,), jnp.float32, math.log(0.15), math.log(0.6))), 0.15, 0.6)
    out_scale = jnp.clip(jax.random.uniform(seeds[2], (1,), jnp.float32, 0.5, 2.0), 0.5, 2.0)
    noise = jnp.clip(jax.random.uniform(seeds[3], (1,), jnp.float32, 0.5, 1.5), 0.5, 1.5)
    solution = bell_draw(seeds[4], (VEC, NPTS), 1.0, 6.0, ((1, 128),), jnp.float32)
    residual = bell_draw(seeds[5], (VEC, NPTS), 1.0, 6.0, ((1, 128),), jnp.float32)
    direction = bell_draw(seeds[6], (VEC, NPTS), 1.0, 6.0, ((1, 128),), jnp.float32)
    return dict(points=points, inv_length=inv_length, out_scale=out_scale, noise=noise, solution=solution, residual=residual, direction=direction)


HIGH = lax.Precision.HIGHEST

def kernel_tile(rows_scaled, rows_sq, cols_scaled, out_scale):
    cols_sq = lax.optimization_barrier(jnp.sum(cols_scaled * cols_scaled, axis=0))
    cross = lax.dot_general(rows_scaled, cols_scaled, (((0,), (0,)), ((), ())), precision=HIGH)
    dist_sq = jnp.maximum(rows_sq[:, None] + cols_sq[None, :] - 2.0 * cross, 0.0)
    radius = jnp.sqrt(5.0 * dist_sq)
    return out_scale[0] * (1.0 + radius + radius * radius / 3.0) * jnp.exp(-radius)

def forward(tile, col_vectors):
    return lax.dot_general(col_vectors, tile, (((1,), (1,)), ((), ())), precision=HIGH)

def reference(points, inv_length, out_scale, noise, solution, residual, direction):
    scaled = points * inv_length[:, None]
    sq = lax.optimization_barrier(jnp.sum(scaled * scaled, axis=0))
    blk = 1024 if NPTS % 1024 == 0 else NPTS
    count = NPTS // blk

    def apply_kernel(vectors):

        def one_block(index):
            start = index * blk
            rows = lax.dynamic_slice_in_dim(scaled, start, blk, 1)
            rows_sq = lax.dynamic_slice_in_dim(sq, start, blk, 0)
            tile = kernel_tile(rows, rows_sq, scaled, out_scale)
            return forward(tile, vectors)
        pieces = lax.map(one_block, jnp.arange(count, dtype=jnp.int32))
        return jnp.transpose(pieces, (1, 0, 2)).reshape(VEC, NPTS) + noise[0] * vectors
    norm_now = lax.optimization_barrier(jnp.sum(residual * residual, axis=1))
    for step in range(ITERS):
        image = apply_kernel(direction)
        alpha = norm_now / lax.optimization_barrier(jnp.sum(direction * image, axis=1))
        solution = solution + alpha[:, None] * direction
        residual = residual - alpha[:, None] * image
        norm_next = lax.optimization_barrier(jnp.sum(residual * residual, axis=1))
        direction = residual + (norm_next / norm_now)[:, None] * direction
        norm_now = norm_next
    return (solution, residual, direction)
```

```python
import functools
import math
import random

import jax
import jax.numpy as jnp
from jax import lax
from jax.experimental import pallas as pl
from jax.experimental.pallas import tpu as pltpu
from jax.sharding import PartitionSpec as P

MESH = pl.DeviceIdType.MESH
f32 = jnp.float32
bf16 = jnp.bfloat16

FEAT = 11
VEC = 8
COLS = 256
CHIPS = 64
GROUP = 8
LOG2E = math.log2(math.e)
LIFT = 1.5 * LOG2E
SHIFT = 0.75 * LOG2E * LOG2E
SCALE = math.exp(1.5) / (3.0 * LOG2E * LOG2E)


def hops(off):
    return sum((0, 1, 2, 1)[d] for d in off)


def offsets():
    every = [(i, j, k) for i in range(4) for j in range(4) for k in range(4)]
    random.Random(1).shuffle(every)
    return sorted(every, key=hops)


OFFS = offsets()


def split3(rows):
    high = rows.astype(bf16)
    rest = rows - high.astype(f32)
    mid = rest.astype(bf16)
    low = (rest - mid.astype(f32)).astype(bf16)
    return high, mid, low


def col_stack(rows):
    h, m, l = split3(rows)
    return jnp.concatenate([h, h, m, m, h, l, jnp.zeros((32, rows.shape[1]), bf16)], 0)


def row_stack(rows):
    h, m, l = split3(rows)
    return jnp.concatenate([h, m, h, m, l, h, jnp.zeros((32, rows.shape[1]), bf16)], 0)


def vec_stack(rows):
    high = rows.astype(bf16).astype(f32)
    return jnp.concatenate([high, rows - high], 0).astype(bf16)


def tile_of(t):
    t = jnp.maximum(t, 1e-30)
    w = -LIFT - t * lax.rsqrt(t)
    return (w * w + SHIFT) * jnp.exp2(w)


def mv(x, k):
    return jnp.dot(x, k, preferred_element_type=f32)


def fold(acc):
    return acc[0:VEC] + acc[VEC : 2 * VEC]


def kernel(
    pts, inv, oscale, noise, sol, res, dirn,
    sol_out, res_out, dir_out,
    snd, rsnd, isnd, fsnd, gath, rgath, igath, fgath,
    qmat, khi, klo, acc_d, acc_r, acc_i, dots,
    ex_s, ex_p, ex_a, ex_b, ex_c, ex_d, ex_e,
    s_p, r_p, s_r, r_r, s_i, r_i, s_f, r_f, s_x, r_x,
):
    g, m = lax.axis_index("grp"), lax.axis_index("mem")
    x, y, z, core = g // 8, (g // 2) % 4, (m // 2) * 2 + g % 2, m % 2
    xs = [((x + d) % 4) * 8 for d in range(4)]
    ys = [((y + d) % 4) * 2 for d in range(4)]
    zs = [(z + d) % 4 for d in range(4)]
    zg = [v % 2 for v in zs]
    zm = [(v // 2) * 2 + core for v in zs]
    partner = (g, (m // 2) * 2 + 1 - core)

    def peer(k):
        dx, dy, dz = OFFS[k]
        return (xs[dx] + ys[dy] + zg[dz], zm[dz])

    barrier = pltpu.get_barrier_semaphore()
    pl.semaphore_signal(barrier, inc=1, device_id=partner, device_id_type=MESH)
    for k in range(1, CHIPS):
        pl.semaphore_signal(barrier, inc=1, device_id=peer(k), device_id_type=MESH)

    gain = math.sqrt(5.0) * LOG2E
    snd[...] = jnp.zeros_like(snd)
    for f in range(FEAT):
        snd[f : f + 1, :] = pts[f : f + 1, :] * (inv[f] * gain)
    scaled = snd[0:16, :]
    snd[11:12, :] = jnp.sum(scaled * scaled, axis=0, keepdims=True)
    snd[12:13, :] = jnp.ones((1, COLS), f32)
    snd[16:24, :] = dirn[...]
    rsnd[...] = res[...]

    def exchange(n, src, dst):
        cp = pltpu.make_async_remote_copy(
            src_ref=src, dst_ref=dst, send_sem=s_x.at[n], recv_sem=r_x.at[n],
            device_id=partner, device_id_type=MESH,
        )
        cp.start()
        return cp

    def spread(src, dst, s, r, start=True):
        own = pltpu.make_async_copy(src, dst.at[0], r.at[0])
        cps = [own]
        for k in range(1, CHIPS):
            cps.append(
                pltpu.make_async_remote_copy(
                    src_ref=src, dst_ref=dst.at[k], send_sem=s.at[k], recv_sem=r.at[k],
                    device_id=peer(k), device_id_type=MESH,
                )
            )
        for cp in cps:
            cp.start()

    def arrived(grp, src, dst, s, r):
        for u in range(GROUP):
            k = grp * GROUP + u
            pltpu.make_async_copy(src, dst.at[k], r.at[k]).wait()

    def sent(src, dst, s, r):
        for k in range(1, CHIPS):
            pltpu.make_async_copy(src, dst.at[k], s.at[k]).wait()

    pl.semaphore_wait(barrier, CHIPS)
    cp_p = exchange(0, snd.at[pl.ds(0, 16)], ex_p)
    spread(snd, gath, s_p, r_p)
    spread(rsnd, rgath, s_r, r_r)

    row = lax.broadcasted_iota(jnp.int32, (16, COLS), 0)

    def rows_side(blk):
        swapped = jnp.where(row == 11, 1.0, jnp.where(row == 12, blk[11:12, :], 0.0))
        return row_stack(jnp.where(row < FEAT, -2.0 * blk, swapped))

    qmat[:, 0:COLS] = rows_side(snd[0:16, :])
    cp_p.wait()
    qmat[:, COLS : 2 * COLS] = rows_side(ex_p[...])

    acc_d[...] = jnp.zeros_like(acc_d)
    acc_r[...] = jnp.zeros_like(acc_r)
    acc_i[...] = jnp.zeros_like(acc_i)
    dots[...] = jnp.zeros_like(dots)

    @pl.loop(0, CHIPS // GROUP)
    def _(grp):
        arrived(grp, snd, gath, s_p, r_p)
        for u in range(GROUP):
            k = grp * GROUP + u
            cols = col_stack(gath[k, 0:16, :])
            vec = vec_stack(gath[k, 16:24, :])
            for i0 in range(0, 2 * COLS, 256):
                part = acc_d[:, i0 : i0 + 256]
                for j0 in range(0, COLS, 128):
                    t = lax.dot_general(
                        cols[:, j0 : j0 + 128], qmat[:, i0 : i0 + 256],
                        (((0,), (0,)), ((), ())), preferred_element_type=f32,
                    )
                    tile = tile_of(t)
                    hi = tile.astype(bf16)
                    lo = (tile - hi.astype(f32)).astype(bf16)
                    khi[k, j0 : j0 + 128, i0 : i0 + 256] = hi
                    klo[k, j0 : j0 + 128, i0 : i0 + 256] = lo
                    v = vec[:, j0 : j0 + 128]
                    part = part + mv(v, hi) + mv(v, lo)
                acc_d[:, i0 : i0 + 256] = part

    def times(acc, src, grp):
        for i0 in range(0, 2 * COLS, 256):
            part = acc[:, i0 : i0 + 256]
            for u in range(GROUP):
                k = grp * GROUP + u
                v = vec_stack(src[k])
                part = part + mv(v, khi[k, :, i0 : i0 + 256]) + mv(v, klo[k, :, i0 : i0 + 256])
            acc[:, i0 : i0 + 256] = part

    total = fold(acc_d[...])
    ex_s[...] = total[:, COLS:]
    cp_a = exchange(1, ex_s, ex_a)
    cp_a.wait()
    kd = (SCALE * oscale[0]) * (total[:, :COLS] + ex_a[...])
    image = kd + noise[0] * dirn[...]
    isnd[...] = image
    spread(isnd, igath, s_i, r_i)

    @pl.loop(0, CHIPS // GROUP)
    def _(grp):
        arrived(grp, rsnd, rgath, s_r, r_r)
        times(acc_r, rgath, grp)

    sent(snd, gath, s_p, r_p)
    sent(rsnd, rgath, s_r, r_r)

    @pl.loop(0, CHIPS // GROUP)
    def _(grp):
        arrived(grp, isnd, igath, s_i, r_i)
        rr, di = dots[0], dots[1]
        for u in range(GROUP):
            k = grp * GROUP + u
            r, d, im = rgath[k], gath[k, 16:24, :], igath[k]
            rr = rr + r * r
            di = di + d * im
        dots[0] = rr
        dots[1] = di
        times(acc_i, igath, grp)

    lane = lax.broadcasted_iota(jnp.int32, (VEC, 128), 1)

    def pack(*cols):
        out = jnp.zeros((VEC, 128), f32)
        for n, c in enumerate(cols):
            out = jnp.where(lane == n, c, out)
        return out

    def take(a, n):
        return jnp.sum(jnp.where(lane == n, a, 0.0), axis=1, keepdims=True)

    def total_of(a):
        return jnp.sum(a, axis=1, keepdims=True)

    mine = pack(total_of(dots[0]), total_of(dots[1]))
    fsnd[0] = mine
    cp_b = exchange(2, fsnd.at[0], ex_b)
    cp_b.wait()
    both = mine + ex_b[...]
    norm0 = take(both, 0)
    alpha0 = norm0 / take(both, 1)

    def sq_step(k, acc):
        r1 = rgath[k] - alpha0 * igath[k]
        return acc + r1 * r1

    mine = pack(total_of(lax.fori_loop(0, CHIPS, sq_step, jnp.zeros((VEC, COLS), f32))))
    fsnd[1] = mine
    cp_c = exchange(3, fsnd.at[1], ex_c)
    part = fold(acc_r[...]) - alpha0 * fold(acc_i[...])
    ex_s2 = ex_d.at[0]
    ex_s2[...] = part[:, COLS:]
    cp_d = exchange(4, ex_s2, ex_d.at[1])
    cp_c.wait()
    norm1 = take(mine + ex_c[...], 0)
    beta = norm1 / norm0
    r1 = res[...] - alpha0 * image
    d1 = r1 + beta * dirn[...]
    cp_d.wait()
    im1 = (SCALE * oscale[0]) * (part[:, :COLS] + ex_d[1]) + beta * kd + noise[0] * d1
    mine = pack(total_of(d1 * im1), total_of(r1 * im1), total_of(im1 * im1))
    fsnd[2] = mine
    spread(fsnd.at[2], fgath, s_f, r_f)

    sent(isnd, igath, s_i, r_i)
    sol1 = sol[...] + alpha0 * dirn[...]

    for grp in range(CHIPS // GROUP):
        arrived(grp, fsnd.at[2], fgath, s_f, r_f)
    mine = jnp.sum(fgath[...], axis=0)
    fsnd[3] = mine
    cp_e = exchange(5, fsnd.at[3], ex_e)
    cp_e.wait()
    both = mine + ex_e[...]
    alpha1 = norm1 / take(both, 0)
    norm2 = norm1 + alpha1 * (alpha1 * take(both, 2) - 2.0 * take(both, 1))
    r2 = r1 - alpha1 * im1
    sol_out[...] = sol1 + alpha1 * d1
    res_out[...] = r2
    dir_out[...] = r2 + (norm2 / norm1) * d1
    sent(fsnd.at[2], fgath, s_f, r_f)


def per_device(points, inv_length, out_scale, noise, solution, residual, direction):
    vm = pl.BlockSpec(memory_space=pltpu.VMEM)
    sm = pl.BlockSpec(memory_space=pltpu.SMEM)
    out = jax.ShapeDtypeStruct((VEC, COLS), f32)
    V, D = pltpu.VMEM, pltpu.SemaphoreType.DMA
    return pl.pallas_call(
        kernel,
        out_shape=(out, out, out),
        in_specs=[vm, sm, sm, sm, vm, vm, vm],
        out_specs=(vm, vm, vm),
        scratch_shapes=[
            V((24, COLS), f32), V((VEC, COLS), f32), V((VEC, COLS), f32), V((4, VEC, 128), f32),
            V((CHIPS, 24, COLS), f32), V((CHIPS, VEC, COLS), f32),
            V((CHIPS, VEC, COLS), f32), V((CHIPS, VEC, 128), f32),
            V((128, 2 * COLS), bf16),
            V((CHIPS, COLS, 2 * COLS), bf16), V((CHIPS, COLS, 2 * COLS), bf16),
            V((16, 2 * COLS), f32), V((16, 2 * COLS), f32), V((16, 2 * COLS), f32),
            V((2, VEC, COLS), f32),
            V((VEC, COLS), f32), V((16, COLS), f32), V((VEC, COLS), f32),
            V((VEC, 128), f32), V((VEC, 128), f32), V((2, VEC, COLS), f32), V((VEC, 128), f32),
            D((CHIPS,)), D((CHIPS,)), D((CHIPS,)), D((CHIPS,)),
            D((CHIPS,)), D((CHIPS,)), D((CHIPS,)), D((CHIPS,)),
            D((6,)), D((6,)),
        ],
        compiler_params=pltpu.CompilerParams(
            collective_id=0, has_side_effects=True, vmem_limit_bytes=56 * 2**20
        ),
        name="cg",
    )(points, inv_length, out_scale, noise, solution, residual, direction)


def solution(mesh):
    cols = P(None, ("grp", "mem"))
    return jax.shard_map(
        per_device,
        mesh=mesh,
        in_specs=(cols, P(), P(), P(), cols, cols, cols),
        out_specs=(cols, cols, cols),
        check_vma=False,
    )
```

```python
import math
import random

import jax
import jax.numpy as jnp
from jax import lax
from jax.experimental import pallas as pl
from jax.experimental.pallas import tpu as pltpu
from jax.sharding import PartitionSpec as P

MESH = pl.DeviceIdType.MESH
f32 = jnp.float32
bf16 = jnp.bfloat16

FEAT = 11
VEC = 8
COLS = 256
CHIPS = 64
GROUPS = 7
LOG2E = math.log2(math.e)
LIFT = 1.5 * LOG2E
SHIFT = 0.75 * LOG2E * LOG2E
SCALE = math.exp(1.5) / (3.0 * LOG2E * LOG2E)


def offsets():
    every = [(i, j, k) for k in range(4) for j in range(4) for i in range(4)]
    random.Random(1).shuffle(every)
    return sorted(every, key=lambda o: -sum((0, 1, 2, 1)[d] for d in o))[:-1]


OFFS = offsets()


def split3(rows):
    high = rows.astype(bf16)
    rest = rows - high.astype(f32)
    mid = rest.astype(bf16)
    low = (rest - mid.astype(f32)).astype(bf16)
    return high, mid, low


def col_stack(rows):
    h, m, l = split3(rows)
    return jnp.concatenate([h, h, m, m, h, l, jnp.zeros((32, rows.shape[1]), bf16)], 0)


def row_stack(rows):
    h, m, l = split3(rows)
    return jnp.concatenate([h, m, h, m, l, h, jnp.zeros((32, rows.shape[1]), bf16)], 0)


def vec_stack(rows):
    high = rows.astype(bf16).astype(f32)
    return jnp.concatenate([high, rows - high], 0).astype(bf16)


def tile_of(t):
    t = jnp.maximum(t, 1e-30)
    w = -LIFT - t * lax.rsqrt(t)
    return (w * w + SHIFT) * jnp.exp2(w)


def mv(x, k):
    return jnp.dot(x, k, preferred_element_type=f32)


def fold(acc):
    return acc[0:VEC] + acc[VEC : 2 * VEC]


def kernel(
    pts, inv, oscale, noise, sol, res, dirn,
    sol_out, res_out, dir_out,
    gath, igath, fgath, isnd, fsnd,
    qmat, khi, klo, acc_d, acc_r, acc_i, dots,
    ex_p, ex_s, ex_r, sc_s, sc_r,
    s_line, r_line, s_run, r_run, s_one, r_one,
    s_i, r_i, s_f, r_f, s_x, r_x,
):
    g, m = lax.axis_index("grp"), lax.axis_index("mem")
    x, y, z, core = g // 8, (g // 2) % 4, (m // 2) * 2 + g % 2, m % 2
    partner = (g, (m // 2) * 2 + 1 - core)

    def peer(e1, e2, e3):
        px = (x + e1 + core * (e3 - e1)) % 4
        py = (y + e2) % 4
        pz = (z + e3 + core * (e1 - e3)) % 4
        return ((px * 4 + py) * 2 + pz % 2, (pz // 2) * 2 + core)

    barrier = pltpu.get_barrier_semaphore()

    def greet(device):
        pl.semaphore_signal(barrier, inc=1, device_id=device, device_id_type=MESH)

    greet(partner)
    for e in (1, 3, 2):
        greet(peer(e, 0, 0))
        greet(peer(0, e, 0))
        greet(peer(0, 0, e))

    gain = math.sqrt(5.0) * LOG2E
    own = gath.at[0, 0, 0]
    own[0:16, :] = jnp.zeros((16, COLS), f32)
    for f in range(FEAT):
        own[f : f + 1, :] = pts[f : f + 1, :] * (inv[f] * gain)
    scaled = own[0:16, :]
    own[11:12, :] = jnp.sum(scaled * scaled, axis=0, keepdims=True)
    own[12:13, :] = jnp.ones((1, COLS), f32)
    own[16:24, :] = dirn[...]
    own[24:32, :] = res[...]

    def put(src, dst, s, r, device):
        cp = pltpu.make_async_remote_copy(
            src_ref=src, dst_ref=dst, send_sem=s, recv_sem=r, device_id=device, device_id_type=MESH
        )
        cp.start()
        return cp

    def await_(ref, sem):
        pltpu.make_async_copy(ref, ref, sem).wait()

    def exchange(n, src, dst):
        return put(src, dst, s_x.at[n], r_x.at[n], partner)

    def run(e3, e2):
        return gath.at[e3, e2, pl.ds(1, 3)]

    def one(e3, e2):
        return gath.at[e3, e2, 0]

    pl.semaphore_wait(barrier, 10)
    cp_p = exchange(0, own.at[pl.ds(0, 16)], ex_p)
    for e in (1, 3, 2):
        put(own, gath.at[0, 0, e], s_line.at[e], r_line.at[e], peer(e, 0, 0))
        put(own, one(0, e), s_one.at[e], r_one.at[e], peer(0, e, 0))
        put(own, one(e, 0), s_one.at[4 * e], r_one.at[4 * e], peer(0, 0, e))

    row = lax.broadcasted_iota(jnp.int32, (16, COLS), 0)

    def rows_side(blk):
        swapped = jnp.where(row == 11, 1.0, jnp.where(row == 12, blk[11:12, :], 0.0))
        return row_stack(jnp.where(row < FEAT, -2.0 * blk, swapped))

    acc_d[...] = jnp.zeros_like(acc_d)
    acc_r[...] = jnp.zeros_like(acc_r)
    acc_i[...] = jnp.zeros_like(acc_i)
    dots[...] = jnp.zeros_like(dots)
    qmat[:, 0:COLS] = rows_side(own[0:16, :])
    cp_p.wait()
    qmat[:, COLS : 2 * COLS] = rows_side(ex_p[...])

    def build(places):
        for e3, e2, e1 in places:
            k = e3 * 16 + e2 * 4 + e1
            cols = col_stack(gath[e3, e2, e1, 0:16, :])
            vec = vec_stack(gath[e3, e2, e1, 16:24, :])
            for i0 in range(0, 2 * COLS, 256):
                part = acc_d[:, i0 : i0 + 256]
                for j0 in range(0, COLS, 128):
                    t = lax.dot_general(
                        cols[:, j0 : j0 + 128], qmat[:, i0 : i0 + 256],
                        (((0,), (0,)), ((), ())), preferred_element_type=f32,
                    )
                    tile = tile_of(t)
                    hi = tile.astype(bf16)
                    lo = (tile - hi.astype(f32)).astype(bf16)
                    khi[k, j0 : j0 + 128, i0 : i0 + 256] = hi
                    klo[k, j0 : j0 + 128, i0 : i0 + 256] = lo
                    v = vec[:, j0 : j0 + 128]
                    part = part + mv(v, hi) + mv(v, lo)
                acc_d[:, i0 : i0 + 256] = part

    def times(acc, places, rows_of):
        for i0 in range(0, 2 * COLS, 256):
            part = acc[:, i0 : i0 + 256]
            for e3, e2, e1 in places:
                k = e3 * 16 + e2 * 4 + e1
                v = vec_stack(rows_of(e3, e2, e1))
                part = part + mv(v, khi[k, :, i0 : i0 + 256]) + mv(v, klo[k, :, i0 : i0 + 256])
            acc[:, i0 : i0 + 256] = part

    def pick(grp, *cases):
        out = cases[-1]
        for n in range(len(cases) - 2, -1, -1):
            out = jnp.where(grp == n, cases[n], out)
        return out

    def third(grp):
        return pick(grp, 0, 0, 0, 0, 1, 3, 2)

    def places_of(grp):
        e = third(grp)
        return [
            (
                pick(grp, p if q == 3 else 0, 0, q, q, e),
                pick(grp, p if q == 2 else 0, q, 0, p, q),
                pick(grp, p if q == 1 else 0, p, p, 0, p),
            )
            for q in range(1, 4)
            for p in range(1, 4)
        ]

    build([(0, 0, 0)])

    for e in (1, 3, 2):
        await_(own, r_line.at[e])
    for e in (1, 3, 2):
        put(run(0, 0), run(0, e), s_run.at[e], r_run.at[e], peer(0, e, 0))
        put(run(0, 0), run(e, 0), s_run.at[4 * e], r_run.at[4 * e], peer(0, 0, e))
    for e in (1, 3, 2):
        await_(own, r_one.at[e])
        for f in (1, 3, 2):
            put(one(0, e), one(f, e), s_one.at[4 * f + e], r_one.at[4 * f + e], peer(0, 0, f))
    for e in (1, 3, 2):
        await_(own, r_one.at[4 * e])

    @pl.loop(0, GROUPS)
    def _(grp):
        @pl.when(grp == 1)
        def _():
            for e in (1, 3, 2):
                await_(run(0, e), r_run.at[e])
                for f in (1, 3, 2):
                    put(run(0, e), run(f, e), s_run.at[4 * f + e], r_run.at[4 * f + e], peer(0, 0, f))

        @pl.when(grp == 2)
        def _():
            for e in (1, 3, 2):
                await_(run(e, 0), r_run.at[4 * e])

        @pl.when(grp == 3)
        def _():
            for e in (1, 3, 2):
                for f in (1, 3, 2):
                    await_(own, r_one.at[4 * e + f])

        @pl.when(grp >= 4)
        def _():
            e = third(grp)
            for f in (1, 3, 2):
                await_(run(e, f), r_run.at[4 * e + f])

        build(places_of(grp))

    total = fold(acc_d[...])
    ex_s[0] = total[:, COLS:]
    cp_a = exchange(1, ex_s.at[0], ex_r.at[0])
    times(acc_r, [(0, 0, 0)], lambda e3, e2, e1: gath[e3, e2, e1, 24:32, :])
    cp_a.wait()
    kd = (SCALE * oscale[0]) * (total[:, :COLS] + ex_r[0])
    image = kd + noise[0] * dirn[...]
    isnd[...] = image
    igath[0, 0, 0] = image
    for n, (e1, e2, e3) in enumerate(OFFS):
        put(isnd, igath.at[e3, e2, e1], s_i.at[0], r_i.at[e3 * 16 + e2 * 4 + e1], peer(e1, e2, e3))

    @pl.loop(0, GROUPS)
    def _(grp):
        times(acc_r, places_of(grp), lambda e3, e2, e1: gath[e3, e2, e1, 24:32, :])

    def squares(step):
        def one_step(k, acc):
            v = step(k // 16, (k // 4) % 4, k % 4)
            return acc + v

        return lax.fori_loop(0, CHIPS, one_step, jnp.zeros((VEC, COLS), f32), unroll=8)

    def r_of(e3, e2, e1):
        return gath[e3, e2, e1, 24:32, :]

    dots[0] = squares(lambda *e: r_of(*e) * r_of(*e))
    times(acc_i, [(0, 0, 0)], lambda e3, e2, e1: igath[e3, e2, e1])
    dots[1] = dirn[...] * image

    @pl.loop(0, GROUPS)
    def _(grp):
        places = places_of(grp)
        di = dots[1]
        for e3, e2, e1 in places:
            await_(isnd, r_i.at[e3 * 16 + e2 * 4 + e1])
        for e3, e2, e1 in places:
            di = di + gath[e3, e2, e1, 16:24, :] * igath[e3, e2, e1]
        dots[1] = di
        times(acc_i, places, lambda e3, e2, e1: igath[e3, e2, e1])

    lane = lax.broadcasted_iota(jnp.int32, (VEC, 128), 1)
    sub = lax.broadcasted_iota(jnp.int32, (VEC, 128), 0)

    def pack(*cols):
        out = jnp.zeros((VEC, 128), f32)
        for n, c in enumerate(cols):
            out = jnp.where(lane == n * VEC + sub, c, out)
        return jnp.sum(out, axis=0, keepdims=True)

    def take(a, n):
        return jnp.sum(jnp.where(lane == n * VEC + sub, a, 0.0), axis=1, keepdims=True)

    def total_of(a):
        return jnp.sum(a, axis=1, keepdims=True)

    mine = pack(total_of(dots[0]), total_of(dots[1]))
    sc_s[0] = mine
    cp_b = exchange(2, sc_s.at[0], sc_r.at[0])
    cp_b.wait()
    both = mine + sc_r[0]
    norm0 = take(both, 0)
    alpha0 = norm0 / take(both, 1)

    def r1_sq(e3, e2, e1):
        r1 = r_of(e3, e2, e1) - alpha0 * igath[e3, e2, e1]
        return r1 * r1

    mine = pack(total_of(squares(r1_sq)))
    sc_s[1] = mine
    cp_c = exchange(3, sc_s.at[1], sc_r.at[1])
    part = fold(acc_r[...]) - alpha0 * fold(acc_i[...])
    ex_s[1] = part[:, COLS:]
    cp_d = exchange(4, ex_s.at[1], ex_r.at[1])
    cp_c.wait()
    norm1 = take(mine + sc_r[1], 0)
    beta = norm1 / norm0
    r1 = res[...] - alpha0 * image
    d1 = r1 + beta * dirn[...]
    cp_d.wait()
    im1 = (SCALE * oscale[0]) * (part[:, :COLS] + ex_r[1]) + beta * kd + noise[0] * d1
    mine = pack(total_of(d1 * im1), total_of(r1 * im1), total_of(im1 * im1))
    fsnd[...] = mine
    fgath[0] = mine
    for n, (e1, e2, e3) in enumerate(OFFS):
        k = e3 * 16 + e2 * 4 + e1
        put(fsnd, fgath.at[k], s_f.at[0], r_f.at[k], peer(e1, e2, e3))

    sol1 = sol[...] + alpha0 * dirn[...]
    for e in range(1, 4):
        await_(own, s_line.at[e])
    for e in range(1, 16):
        await_(own, s_one.at[e])
        await_(run(0, 0), s_run.at[e])
    flat = igath.at[pl.ds(1, 3)], igath.at[0, pl.ds(1, 3)], igath.at[0, 0, pl.ds(1, 3)]
    for ref in flat:
        await_(ref, s_i.at[0])

    for k in range(1, CHIPS):
        await_(fsnd, r_f.at[k])
    mine = jnp.sum(fgath[...], axis=0)
    sc_s[2] = mine
    cp_e = exchange(5, sc_s.at[2], sc_r.at[2])
    cp_e.wait()
    both = mine + sc_r[2]
    alpha1 = norm1 / take(both, 0)
    norm2 = norm1 + alpha1 * (alpha1 * take(both, 2) - 2.0 * take(both, 1))
    r2 = r1 - alpha1 * im1
    sol_out[...] = sol1 + alpha1 * d1
    res_out[...] = r2
    dir_out[...] = r2 + (norm2 / norm1) * d1
    await_(fgath.at[pl.ds(1, CHIPS - 1)], s_f.at[0])


def per_device(points, inv_length, out_scale, noise, solution, residual, direction):
    vm = pl.BlockSpec(memory_space=pltpu.VMEM)
    sm = pl.BlockSpec(memory_space=pltpu.SMEM)
    out = jax.ShapeDtypeStruct((VEC, COLS), f32)
    V, D = pltpu.VMEM, pltpu.SemaphoreType.DMA
    return pl.pallas_call(
        kernel,
        out_shape=(out, out, out),
        in_specs=[vm, sm, sm, sm, vm, vm, vm],
        out_specs=(vm, vm, vm),
        scratch_shapes=[
            V((4, 4, 4, 32, COLS), f32), V((4, 4, 4, VEC, COLS), f32), V((CHIPS, 1, 128), f32),
            V((VEC, COLS), f32), V((1, 128), f32),
            V((128, 2 * COLS), bf16),
            V((CHIPS, COLS, 2 * COLS), bf16), V((CHIPS, COLS, 2 * COLS), bf16),
            V((16, 2 * COLS), f32), V((16, 2 * COLS), f32), V((16, 2 * COLS), f32),
            V((2, VEC, COLS), f32),
            V((16, COLS), f32), V((2, VEC, COLS), f32), V((2, VEC, COLS), f32),
            V((3, 1, 128), f32), V((3, 1, 128), f32),
            D((4,)), D((4,)), D((16,)), D((16,)), D((16,)), D((16,)),
            D((1,)), D((CHIPS,)), D((1,)), D((CHIPS,)), D((6,)), D((6,)),
        ],
        compiler_params=pltpu.CompilerParams(
            collective_id=0, has_side_effects=True, vmem_limit_bytes=56 * 2**20
        ),
        name="cg",
    )(points, inv_length, out_scale, noise, solution, residual, direction)


def solution(mesh):
    cols = P(None, ("grp", "mem"))
    return jax.shard_map(
        per_device,
        mesh=mesh,
        in_specs=(cols, P(), P(), P(), cols, cols, cols),
        out_specs=(cols, cols, cols),
        check_vma=False,
    )
```

```python
import math

import jax
import jax.numpy as jnp
from jax import lax
from jax.experimental import pallas as pl
from jax.experimental.pallas import tpu as pltpu
from jax.sharding import PartitionSpec as P

MESH = pl.DeviceIdType.MESH
f32 = jnp.float32
bf16 = jnp.bfloat16

FEAT = 11
VEC = 8
COLS = 256
HALF = 128
CHIPS = 64
GROUPS = 7
LOG2E = math.log2(math.e)
LIFT = 1.5 * LOG2E
SHIFT = 0.75 * LOG2E * LOG2E
SCALE = math.exp(1.5) / (3.0 * LOG2E * LOG2E)


def offsets():
    three = (2, 3, 1)
    out = [(i, j, k) for k in three for j in three for i in three]
    out += [(0, j, k) for k in three for j in three]
    out += [(i, 0, k) for k in three for i in three]
    out += [(i, j, 0) for j in three for i in three]
    out += [(0, 0, k) for k in three] + [(0, j, 0) for j in three] + [(i, 0, 0) for i in three]
    return out


OFFS = offsets()


def split3(rows):
    high = rows.astype(bf16)
    rest = rows - high.astype(f32)
    mid = rest.astype(bf16)
    low = (rest - mid.astype(f32)).astype(bf16)
    return high, mid, low


def col_stack(rows):
    h, m, l = split3(rows)
    one = jnp.ones((16, HALF), bf16)
    return jnp.concatenate([h, h, m, m, h, l, one, jnp.zeros_like(one)], 0)


def row_stack(rows, sq):
    h, m, l = split3(rows)
    row = lax.broadcasted_iota(jnp.int32, (16, HALF), 0)
    last = jnp.zeros((16, HALF), f32)
    for n, part in enumerate(split3(sq)):
        last = jnp.where(row == n, part.astype(f32), last)
    return jnp.concatenate([h, m, h, m, l, h, last.astype(bf16), jnp.zeros((16, HALF), bf16)], 0)


def vec_stack(rows):
    high = rows.astype(bf16).astype(f32)
    return jnp.concatenate([high, rows - high], 0).astype(bf16)


def tile_of(t):
    t = jnp.maximum(t, 1e-30)
    w = -LIFT - t * lax.rsqrt(t)
    return (w * w + SHIFT) * jnp.exp2(w)


def mv(x, k):
    return jnp.dot(x, k, preferred_element_type=f32)


def fold(acc):
    return acc[0:VEC] + acc[VEC : 2 * VEC]


def kernel(
    pts, inv, scale, noise, sol, res, dirn,
    outs,
    gath, rgath, igath, fgath, isnd, fsnd,
    qtmp, qmat, khi, klo, acc_d, acc_r, acc_i, dots,
    ex_p, ex_s, ex_r, sc_s, sc_r,
    s_line, r_line, s_run, r_run, s_one, r_one,
    s_i, r_i, s_f, r_f, s_x, r_x,
):
    g, m = lax.axis_index("grp"), lax.axis_index("mem")
    x, y, z, core = g // 8, (g // 2) % 4, (m // 2) * 2 + g % 2, m % 2
    partner = (g, (m // 2) * 2 + 1 - core)

    def peer(e1, e2, e3, other=0):
        px = (x + e1 + core * (e3 - e1)) % 4
        py = (y + e2) % 4
        pz = (z + e3 + core * (e1 - e3)) % 4
        return ((px * 4 + py) * 2 + pz % 2, (pz // 2) * 2 + (1 - core if other else core))

    barrier = pltpu.get_barrier_semaphore()

    def greet(device):
        pl.semaphore_signal(barrier, inc=1, device_id=device, device_id_type=MESH)

    greet(partner)
    for e in (1, 3, 2):
        greet(peer(e, 0, 0))
        greet(peer(0, e, 0))
        greet(peer(0, 0, e))

    gain = math.sqrt(5.0) * LOG2E
    own, r_own = gath.at[0, 0, 0], rgath.at[0, 0, 0]
    r_own[...] = res[...]
    for half, (at, at_sq) in enumerate(((16, 27), (29, 28))):
        lanes = slice(half * HALF, (half + 1) * HALF)
        own[8 * half : 8 * half + 8, :] = dirn[:, lanes]
        sq = jnp.zeros((1, HALF), f32)
        for f in range(FEAT):
            scaled = pts[f : f + 1, lanes] * (inv[f] * gain)
            own[at + f : at + f + 1, :] = scaled
            sq = sq + scaled * scaled
        own[at_sq : at_sq + 1, :] = sq

    def put(src, dst, s, r, device):
        cp = pltpu.make_async_remote_copy(
            src_ref=src, dst_ref=dst, send_sem=s, recv_sem=r, device_id=device, device_id_type=MESH
        )
        cp.start()
        return cp

    def await_(ref, sem):
        pltpu.make_async_copy(ref, ref, sem).wait()

    def exchange(n, src, dst):
        return put(src, dst, s_x.at[n], r_x.at[n], partner)

    bufs = gath, rgath

    def run(w, e3, e2):
        return bufs[w].at[e3, e2, pl.ds(1, 3)]

    def one(w, e3, e2):
        return bufs[w].at[e3, e2, 0]

    def put_run(w, src, e3, e2, device):
        n = 4 * e3 + e2
        put(run(w, *src), run(w, e3, e2), s_run.at[w, n], r_run.at[w, n], device)

    def put_one(w, src, e3, e2, device):
        n = 4 * e3 + e2
        put(one(w, *src), one(w, e3, e2), s_one.at[w, n], r_one.at[w, n], device)

    def await_run(w, e3, e2):
        await_(run(w, 0, 0), r_run.at[w, 4 * e3 + e2])

    def await_one(w, e3, e2):
        await_(one(w, 0, 0), r_one.at[w, 4 * e3 + e2])

    def leave(w):
        for e in (1, 3, 2):
            put(one(w, 0, 0), bufs[w].at[0, 0, e], s_line.at[w, e], r_line.at[w, e], peer(e, 0, 0))
            put_one(w, (0, 0), 0, e, peer(0, e, 0))
            put_one(w, (0, 0), e, 0, peer(0, 0, e))

    def pass_lines(w):
        for e in (1, 3, 2):
            await_(one(w, 0, 0), r_line.at[w, e])
        for e in (1, 3, 2):
            put_run(w, (0, 0), 0, e, peer(0, e, 0))
            put_run(w, (0, 0), e, 0, peer(0, 0, e))
        for e in (1, 3, 2):
            await_one(w, 0, e)
            for f in (1, 3, 2):
                put_one(w, (0, e), f, e, peer(0, 0, f))
        for e in (1, 3, 2):
            await_one(w, e, 0)

    def pass_planes(w):
        for e in (1, 3, 2):
            await_run(w, 0, e)
            for f in (1, 3, 2):
                put_run(w, (0, e), f, e, peer(0, 0, f))

    pl.semaphore_wait(barrier, 10)
    cp_p = exchange(0, own.at[pl.ds(16, 24)], ex_p)
    leave(0)
    leave(1)

    def rows_side(blk, top, start):
        for half, (at, at_sq) in enumerate(((16, 27), (29, 28))):
            p = -2.0 * blk[at - top : at - top + FEAT, :]
            sq = blk[at_sq - top : at_sq - top + 1, :]
            for cols, (put_at, one_at) in enumerate(((0, 11), (5, 4))):
                qtmp[...] = jnp.zeros_like(qtmp)
                qtmp[put_at : put_at + FEAT, :] = p
                qtmp[one_at : one_at + 1, :] = jnp.ones((1, HALF), f32)
                lanes = slice(start + half * HALF, start + (half + 1) * HALF)
                qmat[cols, :, lanes] = row_stack(qtmp[...], sq)

    for acc in (acc_d, acc_r, acc_i):
        acc[...] = jnp.zeros_like(acc)
    rows_side(own, 0, 0)
    cp_p.wait()
    rows_side(ex_p, 16, COLS)

    def build(places):
        for e3, e2, e1 in places:
            k = e3 * 16 + e2 * 4 + e1
            blk = gath.at[e3, e2, e1]
            cols = col_stack(blk[16:32, :]), col_stack(blk[24:40, :])
            vec = vec_stack(blk[0:8, :]), vec_stack(blk[8:16, :])
            for i0 in range(0, 2 * COLS, 256):
                part = acc_d[:, i0 : i0 + 256]
                for half in (0, 1):
                    j0 = half * HALF
                    t = lax.dot_general(
                        cols[half], qmat[half, :, i0 : i0 + 256],
                        (((0,), (0,)), ((), ())), preferred_element_type=f32,
                    )
                    tile = tile_of(t)
                    hi = tile.astype(bf16)
                    lo = (tile - hi.astype(f32)).astype(bf16)
                    khi[k, j0 : j0 + HALF, i0 : i0 + 256] = hi
                    klo[k, j0 : j0 + HALF, i0 : i0 + 256] = lo
                    part = part + mv(vec[half], hi) + mv(vec[half], lo)
                acc_d[:, i0 : i0 + 256] = part

    def times(acc, places, rows_of):
        for i0 in range(0, 2 * COLS, 256):
            part = acc[:, i0 : i0 + 256]
            for e3, e2, e1 in places:
                k = e3 * 16 + e2 * 4 + e1
                v = vec_stack(rows_of(e3, e2, e1))
                part = part + mv(v, khi[k, :, i0 : i0 + 256]) + mv(v, klo[k, :, i0 : i0 + 256])
            acc[:, i0 : i0 + 256] = part

    def pick(grp, *cases):
        out = cases[-1]
        for n in range(len(cases) - 2, -1, -1):
            out = jnp.where(grp == n, cases[n], out)
        return out

    def third(grp):
        return pick(grp, 0, 0, 0, 0, 1, 3, 2)

    def places_of(grp):
        e = third(grp)
        return [
            (
                pick(grp, p if q == 3 else 0, 0, q, q, e),
                pick(grp, p if q == 2 else 0, q, 0, p, q),
                pick(grp, p if q == 1 else 0, p, p, 0, p),
            )
            for q in range(1, 4)
            for p in range(1, 4)
        ]

    build([(0, 0, 0)])

    pass_lines(0)

    @pl.loop(0, GROUPS)
    def _(grp):
        @pl.when(grp == 1)
        def _():
            pass_planes(0)
            pass_lines(1)

        @pl.when(grp == 2)
        def _():
            for e in (1, 3, 2):
                await_run(0, e, 0)

        @pl.when(grp == 3)
        def _():
            for e in (1, 3, 2):
                for f in (1, 3, 2):
                    await_one(0, e, f)
            pass_planes(1)

        @pl.when(grp >= 4)
        def _():
            for f in (1, 3, 2):
                await_run(0, third(grp), f)

        build(places_of(grp))

    total = fold(acc_d[...])
    ex_s[0] = total[:, COLS:]
    cp_a = exchange(1, ex_s.at[0], ex_r.at[0])
    times(acc_r, [(0, 0, 0)], lambda e3, e2, e1: rgath[e3, e2, e1])
    cp_a.wait()
    kd = (SCALE * scale[0]) * (total[:, :COLS] + ex_r[0])
    image = kd + noise[0] * dirn[...]
    isnd[...] = image
    igath[0, 0, 0] = image
    for n, (e1, e2, e3) in enumerate(OFFS):
        put(isnd, igath.at[e3, e2, e1], s_i.at[0], r_i.at[e3 * 16 + e2 * 4 + e1], peer(e1, e2, e3))

    for e in (1, 3, 2):
        await_run(1, e, 0)
        for f in (1, 3, 2):
            await_one(1, e, f)
            await_run(1, e, f)

    @pl.loop(0, GROUPS)
    def _(grp):
        times(acc_r, places_of(grp), lambda e3, e2, e1: rgath[e3, e2, e1])

    def squares(step):
        def one_step(k, acc):
            v = step(k // 16, (k // 4) % 4, k % 4)
            return acc + v

        return lax.fori_loop(0, CHIPS, one_step, jnp.zeros((VEC, COLS), f32), unroll=8)

    def r_of(e3, e2, e1):
        return rgath[e3, e2, e1]

    rr = squares(lambda *e: r_of(*e) * r_of(*e))
    times(acc_i, [(0, 0, 0)], lambda e3, e2, e1: igath[e3, e2, e1])
    dots[...] = dirn[...] * image

    def meet(places):
        di = dots[...]
        for e3, e2, e1 in places:
            await_(isnd, r_i.at[e3 * 16 + e2 * 4 + e1])
        for e3, e2, e1 in places:
            blk = gath.at[e3, e2, e1]
            d = jnp.concatenate([blk[0:8, :], blk[8:16, :]], 1)
            di = di + d * igath[e3, e2, e1]
        dots[...] = di

    @pl.loop(0, GROUPS - 1)
    def _(back):
        places = places_of(GROUPS - 1 - back)
        meet(places)
        times(acc_i, places, lambda e3, e2, e1: igath[e3, e2, e1])

    lane = lax.broadcasted_iota(jnp.int32, (VEC, 128), 1)
    sub = lax.broadcasted_iota(jnp.int32, (VEC, 128), 0)

    def pack(*cols):
        out = jnp.zeros((VEC, 128), f32)
        for n, c in enumerate(cols):
            out = jnp.where(lane == n * VEC + sub, c, out)
        return jnp.sum(out, axis=0, keepdims=True)

    def take(a, n):
        return jnp.sum(jnp.where(lane == n * VEC + sub, a, 0.0), axis=1, keepdims=True)

    def total_of(a):
        return jnp.sum(a, axis=1, keepdims=True)

    lines = [(k, 0, 0) for k in (2, 3, 1)] + [(0, j, 0) for j in (2, 3, 1)] + [(0, 0, i) for i in (2, 3, 1)]
    meet(lines)
    mine = pack(total_of(rr), total_of(dots[...]))
    sc_s[0] = mine
    cp_b = exchange(2, sc_s.at[0], sc_r.at[0])
    times(acc_i, lines, lambda e3, e2, e1: igath[e3, e2, e1])
    cp_b.wait()
    both = mine + sc_r[0]
    norm0 = take(both, 0)
    alpha0 = norm0 / take(both, 1)

    def r1_sq(e3, e2, e1):
        r1 = r_of(e3, e2, e1) - alpha0 * igath[e3, e2, e1]
        return r1 * r1

    mine = pack(total_of(squares(r1_sq)))
    sc_s[1] = mine
    cp_c = exchange(3, sc_s.at[1], sc_r.at[1])
    part = fold(acc_r[...]) - alpha0 * fold(acc_i[...])
    ex_s[1] = part[:, COLS:]
    cp_d = exchange(4, ex_s.at[1], ex_r.at[1])
    cp_c.wait()
    norm1 = take(mine + sc_r[1], 0)
    beta = norm1 / norm0
    r1 = res[...] - alpha0 * image
    d1 = r1 + beta * dirn[...]
    cp_d.wait()
    im1 = (SCALE * scale[0]) * (part[:, :COLS] + ex_r[1]) + beta * kd + noise[0] * d1
    mine = pack(total_of(d1 * im1), total_of(r1 * im1), total_of(im1 * im1))
    fsnd[...] = mine
    fgath[0] = mine
    for other in (0, 1):
        for e1, e2, e3 in OFFS + [(0, 0, 0)] * other:
            k = other * CHIPS + e3 * 16 + e2 * 4 + e1
            put(fsnd, fgath.at[k], s_f.at[0], r_f.at[k], peer(e1, e2, e3, other))

    sol1 = sol[...] + alpha0 * dirn[...]
    for w in (0, 1):
        for e in range(1, 4):
            await_(one(w, 0, 0), s_line.at[w, e])
        for e in range(1, 16):
            await_(one(w, 0, 0), s_one.at[w, e])
            await_(run(w, 0, 0), s_run.at[w, e])
    flat = igath.at[pl.ds(1, 3)], igath.at[0, pl.ds(1, 3)], igath.at[0, 0, pl.ds(1, 3)]
    for ref in flat:
        await_(ref, s_i.at[0])

    for k in range(1, 2 * CHIPS):
        await_(fsnd, r_f.at[k])
    both = jnp.sum(fgath[...], axis=0)
    alpha1 = norm1 / take(both, 0)
    norm2 = norm1 + alpha1 * (alpha1 * take(both, 2) - 2.0 * take(both, 1))
    r2 = r1 - alpha1 * im1
    outs[0:8, :] = sol1 + alpha1 * d1
    outs[8:16, :] = r2
    outs[16:24, :] = r2 + (norm2 / norm1) * d1
    await_(fgath.at[pl.ds(1, 2 * CHIPS - 1)], s_f.at[0])


def per_device(points, inv_length, out_scale, noise, solution, residual, direction):
    vm = pl.BlockSpec(memory_space=pltpu.VMEM)
    sm = pl.BlockSpec(memory_space=pltpu.SMEM)
    V, D = pltpu.VMEM, pltpu.SemaphoreType.DMA
    out = pl.pallas_call(
        kernel,
        out_shape=jax.ShapeDtypeStruct((3 * VEC, COLS), f32),
        in_specs=[vm, sm, sm, sm, vm, vm, vm],
        out_specs=vm,
        scratch_shapes=[
            V((4, 4, 4, 40, HALF), f32), V((4, 4, 4, VEC, COLS), f32), V((4, 4, 4, VEC, COLS), f32),
            V((2 * CHIPS, 1, 128), f32), V((VEC, COLS), f32), V((1, 128), f32),
            V((16, HALF), f32), V((2, 128, 2 * COLS), bf16),
            V((CHIPS, COLS, 2 * COLS), bf16), V((CHIPS, COLS, 2 * COLS), bf16),
            V((16, 2 * COLS), f32), V((16, 2 * COLS), f32), V((16, 2 * COLS), f32),
            V((VEC, COLS), f32),
            V((24, HALF), f32), V((2, VEC, COLS), f32), V((2, VEC, COLS), f32),
            V((2, 1, 128), f32), V((2, 1, 128), f32),
            D((2, 4)), D((2, 4)), D((2, 16)), D((2, 16)), D((2, 16)), D((2, 16)),
            D((1,)), D((CHIPS,)), D((1,)), D((2 * CHIPS,)), D((5,)), D((5,)),
        ],
        compiler_params=pltpu.CompilerParams(
            collective_id=0, has_side_effects=True, vmem_limit_bytes=56 * 2**20
        ),
        name="cg",
    )(points, inv_length, out_scale, noise, solution, residual, direction)
    return out[0:8], out[8:16], out[16:24]


def solution(mesh):
    cols = P(None, ("grp", "mem"))
    return jax.shard_map(
        per_device,
        mesh=mesh,
        in_specs=(cols, P(), P(), P(), cols, cols, cols),
        out_specs=(cols, cols, cols),
        check_vma=False,
    )
```

```python
import math

import jax
import jax.numpy as jnp
from jax import lax
from jax.experimental import pallas as pl
from jax.experimental.pallas import tpu as pltpu
from jax.sharding import PartitionSpec as P

MESH = pl.DeviceIdType.MESH
f32 = jnp.float32
bf16 = jnp.bfloat16

FEAT = 11
VEC = 8
COLS = 256
HALF = 128
CHIPS = 64
GROUPS = 7
LOG2E = math.log2(math.e)
LIFT = 1.5 * LOG2E
SHIFT = 0.75 * LOG2E * LOG2E
SCALE = math.exp(1.5) / (3.0 * LOG2E * LOG2E)


def offsets():
    three = (2, 3, 1)
    out = [(i, j, k) for k in three for j in three for i in three]
    out += [(0, j, k) for k in three for j in three]
    out += [(i, 0, k) for k in three for i in three]
    out += [(i, j, 0) for j in three for i in three]
    out += [(0, 0, k) for k in three] + [(0, j, 0) for j in three] + [(i, 0, 0) for i in three]
    return out


OFFS = offsets()


def split3(rows):
    high = rows.astype(bf16)
    rest = rows - high.astype(f32)
    mid = rest.astype(bf16)
    low = (rest - mid.astype(f32)).astype(bf16)
    return high, mid, low


def col_stack(rows):
    h, m, l = split3(rows)
    one = jnp.ones((16, HALF), bf16)
    return jnp.concatenate([h, h, m, m, h, l, one, jnp.zeros_like(one)], 0)


def row_stack(rows, sq):
    h, m, l = split3(rows)
    row = lax.broadcasted_iota(jnp.int32, (16, HALF), 0)
    last = jnp.zeros((16, HALF), f32)
    for n, part in enumerate(split3(sq)):
        last = jnp.where(row == n, part.astype(f32), last)
    return jnp.concatenate([h, m, h, m, l, h, last.astype(bf16), jnp.zeros((16, HALF), bf16)], 0)


def vec_stack(rows):
    high = rows.astype(bf16).astype(f32)
    return jnp.concatenate([high, rows - high], 0).astype(bf16)


def tile_of(t):
    t = jnp.maximum(t, 1e-30)
    w = -LIFT - t * lax.rsqrt(t)
    return (w * w + SHIFT) * jnp.exp2(w)


def mv(x, k):
    return jnp.dot(x, k, preferred_element_type=f32)


def fold(acc):
    return acc[0:VEC] + acc[VEC : 2 * VEC]


def kernel(
    pts_in, inv, scale, noise, sol_in, res_in, dirn_in,
    outs,
    gath, rgath, igath, fgath, isnd, fsnd,
    qtmp, qmat, khi, klo, acc_d, acc_r, acc_i, dots,
    ex_p, ex_s, ex_r, sc_s, sc_r,
    s_line, r_line, s_run, r_run, s_one, r_one,
    s_i, r_i, s_f, r_f, s_x, r_x, s_alt, r_alt,
    pts, sol, res, dirn, s_in,
):
    g, m = lax.axis_index("grp"), lax.axis_index("mem")
    x, y, z, core = g // 8, (g // 2) % 4, (m // 2) * 2 + g % 2, m % 2
    partner = (g, (m // 2) * 2 + 1 - core)

    def peer(e1, e2, e3, other=0):
        px = (x + e1 + core * (e3 - e1)) % 4
        py = (y + e2) % 4
        pz = (z + e3 + core * (e1 - e3)) % 4
        return ((px * 4 + py) * 2 + pz % 2, (pz // 2) * 2 + (1 - core if other else core))

    loads = (pts_in, pts), (dirn_in, dirn), (res_in, res), (sol_in, sol)
    loads = [pltpu.make_async_copy(a, b, s_in.at[n]) for n, (a, b) in enumerate(loads)]
    for cp in loads:
        cp.start()
    barrier = pltpu.get_barrier_semaphore()

    def greet(device):
        pl.semaphore_signal(barrier, inc=1, device_id=device, device_id_type=MESH)

    greet(partner)
    for e in (1, 3, 2):
        greet(peer(e, 0, 0))
        greet(peer(0, e, 0))
        greet(peer(0, 0, e))

    gain = math.sqrt(5.0) * LOG2E
    own, r_own = gath.at[0, 0, 0], rgath.at[0, 0, 0]
    for cp in loads:
        cp.wait()
    r_own[...] = res[...]
    for half, (at, at_sq) in enumerate(((16, 27), (29, 28))):
        lanes = slice(half * HALF, (half + 1) * HALF)
        own[8 * half : 8 * half + 8, :] = dirn[:, lanes]
        sq = jnp.zeros((1, HALF), f32)
        for f in range(FEAT):
            scaled = pts[f : f + 1, lanes] * (inv[f] * gain)
            own[at + f : at + f + 1, :] = scaled
            sq = sq + scaled * scaled
        own[at_sq : at_sq + 1, :] = sq

    def put(src, dst, s, r, device):
        cp = pltpu.make_async_remote_copy(
            src_ref=src, dst_ref=dst, send_sem=s, recv_sem=r, device_id=device, device_id_type=MESH
        )
        cp.start()
        return cp

    def await_(ref, sem):
        pltpu.make_async_copy(ref, ref, sem).wait()

    def exchange(n, src, dst):
        return put(src, dst, s_x.at[n], r_x.at[n], partner)

    bufs = gath, rgath

    def run(w, e3, e2):
        return bufs[w].at[e3, e2, pl.ds(1, 3)]

    def one(w, e3, e2):
        return bufs[w].at[e3, e2, 0]

    def run_from(w, e3, e2):
        return run(w, e3, e2) if 0 in (e3, e2) else bufs[w].at[e3, e2, pl.ds(2, 2)]

    def put_run(w, e3, e2, device):
        src = run(w, 0, 0) if 0 in (e3, e2) else run_from(w, 0, e2).at[pl.ds(1, 2)]
        n = 4 * e3 + e2
        put(src, run_from(w, e3, e2), s_run.at[w, n], r_run.at[w, n], device)

    def put_alt(w, e3, e2, device):
        n = 4 * e3 + e2
        put(bufs[w].at[e3, 0, 1], bufs[w].at[e3, e2, 1], s_alt.at[w, n], r_alt.at[w, n], device)

    def put_one(w, src, e3, e2, device):
        n = 4 * e3 + e2
        put(one(w, *src), one(w, e3, e2), s_one.at[w, n], r_one.at[w, n], device)

    def await_run(w, e3, e2):
        await_(run_from(w, e3, e2), r_run.at[w, 4 * e3 + e2])

    def await_far(w, e3):
        for e2 in (1, 3, 2):
            n = 4 * e3 + e2
            await_(bufs[w].at[0, 0, pl.ds(2, 2)], r_run.at[w, n])
            await_(one(w, 0, 0), r_alt.at[w, n])

    def await_one(w, e3, e2):
        await_(one(w, 0, 0), r_one.at[w, 4 * e3 + e2])

    def leave(w):
        for e in (1, 3, 2):
            put(one(w, 0, 0), bufs[w].at[0, 0, e], s_line.at[w, e], r_line.at[w, e], peer(e, 0, 0))
            put_one(w, (0, 0), 0, e, peer(0, e, 0))
            put_one(w, (0, 0), e, 0, peer(0, 0, e))

    def pass_lines(w):
        for e in (1, 3, 2):
            await_(one(w, 0, 0), r_line.at[w, e])
        for e in (2, 1, 3):
            put_run(w, 0, e, peer(0, e, 0))
        for e in (2, 1, 3):
            put_run(w, e, 0, peer(0, 0, e))
        for e in (1, 3, 2):
            await_one(w, 0, e)
            for f in (2, 1, 3):
                put_one(w, (0, e), f, e, peer(0, 0, f))
        for e in (1, 3, 2):
            await_one(w, e, 0)

    def pass_planes(w):
        for e in (1, 3, 2):
            await_run(w, 0, e)
            for f in (1, 3, 2):
                put_run(w, f, e, peer(0, 0, f))
        for e in (1, 3, 2):
            await_run(w, e, 0)
            for f in (2, 1, 3):
                put_alt(w, e, f, peer(0, f, 0))

    def rows_side(blk, top, start):
        for half, (at, at_sq) in enumerate(((16, 27), (29, 28))):
            p = -2.0 * blk[at - top : at - top + FEAT, :]
            sq = blk[at_sq - top : at_sq - top + 1, :]
            for cols, (put_at, one_at) in enumerate(((0, 11), (5, 4))):
                qtmp[...] = jnp.zeros_like(qtmp)
                qtmp[put_at : put_at + FEAT, :] = p
                qtmp[one_at : one_at + 1, :] = jnp.ones((1, HALF), f32)
                lanes = slice(start + half * HALF, start + (half + 1) * HALF)
                qmat[cols, :, lanes] = row_stack(qtmp[...], sq)

    for acc in (acc_d, acc_r, acc_i):
        acc[...] = jnp.zeros_like(acc)
    rows_side(own, 0, 0)
    pl.semaphore_wait(barrier, 10)
    cp_p = exchange(0, own.at[pl.ds(16, 24)], ex_p)
    leave(0)
    cp_p.wait()
    rows_side(ex_p, 16, COLS)
    def build(places):
        for e3, e2, e1 in places:
            k = e3 * 16 + e2 * 4 + e1
            blk = gath.at[e3, e2, e1]
            cols = col_stack(blk[16:32, :]), col_stack(blk[24:40, :])
            vec = vec_stack(blk[0:8, :]), vec_stack(blk[8:16, :])
            for i0 in range(0, 2 * COLS, 256):
                part = acc_d[:, i0 : i0 + 256]
                for half in (0, 1):
                    j0 = half * HALF
                    t = lax.dot_general(
                        cols[half], qmat[half, :, i0 : i0 + 256],
                        (((0,), (0,)), ((), ())), preferred_element_type=f32,
                    )
                    tile = tile_of(t)
                    hi = tile.astype(bf16)
                    lo = (tile - hi.astype(f32)).astype(bf16)
                    khi[k, j0 : j0 + HALF, i0 : i0 + 256] = hi
                    klo[k, j0 : j0 + HALF, i0 : i0 + 256] = lo
                    part = part + mv(vec[half], hi) + mv(vec[half], lo)
                acc_d[:, i0 : i0 + 256] = part

    def times(acc, places, rows_of):
        for i0 in range(0, 2 * COLS, 256):
            part = acc[:, i0 : i0 + 256]
            for e3, e2, e1 in places:
                k = e3 * 16 + e2 * 4 + e1
                v = vec_stack(rows_of(e3, e2, e1))
                part = part + mv(v, khi[k, :, i0 : i0 + 256]) + mv(v, klo[k, :, i0 : i0 + 256])
            acc[:, i0 : i0 + 256] = part

    def pick(grp, *cases):
        out = cases[-1]
        for n in range(len(cases) - 2, -1, -1):
            out = jnp.where(grp == n, cases[n], out)
        return out

    def third(grp):
        return pick(grp, 0, 0, 0, 0, 1, 3, 2)

    def places_of(grp):
        e = third(grp)
        return [
            (
                pick(grp, p if q == 3 else 0, 0, q, q, e),
                pick(grp, p if q == 2 else 0, q, 0, p, q),
                pick(grp, p if q == 1 else 0, p, p, 0, p),
            )
            for q in range(1, 4)
            for p in range(1, 4)
        ]

    build([(0, 0, 0)])
    pass_lines(0)
    leave(1)

    @pl.loop(0, GROUPS)
    def _(grp):
        @pl.when(grp == 1)
        def _():
            pass_planes(0)
            pass_lines(1)

        @pl.when(grp == 3)
        def _():
            for e in (1, 3, 2):
                for f in (1, 3, 2):
                    await_one(0, e, f)
            pass_planes(1)

        @pl.when(grp >= 4)
        def _():
            await_far(0, third(grp))

        build(places_of(grp))

    total = fold(acc_d[...])
    ex_s[0] = total[:, COLS:]
    cp_a = exchange(1, ex_s.at[0], ex_r.at[0])
    times(acc_r, [(0, 0, 0)], lambda e3, e2, e1: rgath[e3, e2, e1])
    cp_a.wait()
    kd = (SCALE * scale[0]) * (total[:, :COLS] + ex_r[0])
    image = kd + noise[0] * dirn[...]
    isnd[...] = image
    igath[0, 0, 0] = image
    for n, (e1, e2, e3) in enumerate(OFFS):
        put(isnd, igath.at[e3, e2, e1], s_i.at[0], r_i.at[e3 * 16 + e2 * 4 + e1], peer(e1, e2, e3))

    for e in (1, 3, 2):
        await_far(1, e)
        for f in (1, 3, 2):
            await_one(1, e, f)

    @pl.loop(0, GROUPS)
    def _(grp):
        times(acc_r, places_of(grp), lambda e3, e2, e1: rgath[e3, e2, e1])

    def squares(step):
        def one_step(k, acc):
            v = step(k // 16, (k // 4) % 4, k % 4)
            return acc + v

        return lax.fori_loop(0, CHIPS, one_step, jnp.zeros((VEC, COLS), f32), unroll=8)

    def r_of(e3, e2, e1):
        return rgath[e3, e2, e1]

    rr = squares(lambda *e: r_of(*e) * r_of(*e))
    times(acc_i, [(0, 0, 0)], lambda e3, e2, e1: igath[e3, e2, e1])
    dots[...] = dirn[...] * image

    def meet(places):
        di = dots[...]
        for e3, e2, e1 in places:
            await_(isnd, r_i.at[e3 * 16 + e2 * 4 + e1])
        for e3, e2, e1 in places:
            blk = gath.at[e3, e2, e1]
            d = jnp.concatenate([blk[0:8, :], blk[8:16, :]], 1)
            di = di + d * igath[e3, e2, e1]
        dots[...] = di

    @pl.loop(0, GROUPS - 1)
    def _(back):
        places = places_of(GROUPS - 1 - back)
        meet(places)
        times(acc_i, places, lambda e3, e2, e1: igath[e3, e2, e1])

    lane = lax.broadcasted_iota(jnp.int32, (VEC, 128), 1)
    sub = lax.broadcasted_iota(jnp.int32, (VEC, 128), 0)

    def pack(*cols):
        out = jnp.zeros((VEC, 128), f32)
        for n, c in enumerate(cols):
            out = jnp.where(lane == n * VEC + sub, c, out)
        return jnp.sum(out, axis=0, keepdims=True)

    def take(a, n):
        return jnp.sum(jnp.where(lane == n * VEC + sub, a, 0.0), axis=1, keepdims=True)

    def total_of(a):
        return jnp.sum(a, axis=1, keepdims=True)

    lines = [(k, 0, 0) for k in (2, 3, 1)] + [(0, j, 0) for j in (2, 3, 1)] + [(0, 0, i) for i in (2, 3, 1)]
    meet(lines)
    mine = pack(total_of(rr), total_of(dots[...]))
    sc_s[0] = mine
    cp_b = exchange(2, sc_s.at[0], sc_r.at[0])
    times(acc_i, lines, lambda e3, e2, e1: igath[e3, e2, e1])
    cp_b.wait()
    both = mine + sc_r[0]
    norm0 = take(both, 0)
    alpha0 = norm0 / take(both, 1)

    def r1_sq(e3, e2, e1):
        r1 = r_of(e3, e2, e1) - alpha0 * igath[e3, e2, e1]
        return r1 * r1

    mine = pack(total_of(squares(r1_sq)))
    sc_s[1] = mine
    cp_c = exchange(3, sc_s.at[1], sc_r.at[1])
    part = fold(acc_r[...]) - alpha0 * fold(acc_i[...])
    ex_s[1] = part[:, COLS:]
    cp_d = exchange(4, ex_s.at[1], ex_r.at[1])
    cp_c.wait()
    norm1 = take(mine + sc_r[1], 0)
    beta = norm1 / norm0
    r1 = res[...] - alpha0 * image
    d1 = r1 + beta * dirn[...]
    cp_d.wait()
    im1 = (SCALE * scale[0]) * (part[:, :COLS] + ex_r[1]) + beta * kd + noise[0] * d1
    mine = pack(total_of(d1 * im1), total_of(r1 * im1), total_of(im1 * im1))
    fsnd[...] = mine
    fgath[0] = mine
    for other in (0, 1):
        for e1, e2, e3 in OFFS + [(0, 0, 0)] * other:
            k = other * CHIPS + e3 * 16 + e2 * 4 + e1
            put(fsnd, fgath.at[k], s_f.at[0], r_f.at[k], peer(e1, e2, e3, other))

    sol1 = sol[...] + alpha0 * dirn[...]
    for w in (0, 1):
        for e in range(1, 4):
            await_(one(w, 0, 0), s_line.at[w, e])
        for e in range(1, 16):
            await_(one(w, 0, 0), s_one.at[w, e])
            await_(run_from(w, e // 4, e % 4), s_run.at[w, e])
            if e // 4 and e % 4:
                await_(one(w, 0, 0), s_alt.at[w, e])
    flat = igath.at[pl.ds(1, 3)], igath.at[0, pl.ds(1, 3)], igath.at[0, 0, pl.ds(1, 3)]
    for ref in flat:
        await_(ref, s_i.at[0])

    for k in range(1, 2 * CHIPS):
        await_(fsnd, r_f.at[k])
    both = jnp.sum(fgath[...], axis=0)
    alpha1 = norm1 / take(both, 0)
    norm2 = norm1 + alpha1 * (alpha1 * take(both, 2) - 2.0 * take(both, 1))
    r2 = r1 - alpha1 * im1
    outs[0:8, :] = sol1 + alpha1 * d1
    outs[8:16, :] = r2
    outs[16:24, :] = r2 + (norm2 / norm1) * d1
    await_(fgath.at[pl.ds(1, 2 * CHIPS - 1)], s_f.at[0])


def per_device(points, inv_length, out_scale, noise, solution, residual, direction):
    vm = pl.BlockSpec(memory_space=pltpu.VMEM)
    hbm = pl.BlockSpec(memory_space=pl.ANY)
    sm = pl.BlockSpec(memory_space=pltpu.SMEM)
    V, D = pltpu.VMEM, pltpu.SemaphoreType.DMA
    out = pl.pallas_call(
        kernel,
        out_shape=jax.ShapeDtypeStruct((3 * VEC, COLS), f32),
        in_specs=[hbm, sm, sm, sm, hbm, hbm, hbm],
        out_specs=vm,
        scratch_shapes=[
            V((4, 4, 4, 40, HALF), f32), V((4, 4, 4, VEC, COLS), f32), V((4, 4, 4, VEC, COLS), f32),
            V((2 * CHIPS, 1, 128), f32), V((VEC, COLS), f32), V((1, 128), f32),
            V((16, HALF), f32), V((2, 128, 2 * COLS), bf16),
            V((CHIPS, COLS, 2 * COLS), bf16), V((CHIPS, COLS, 2 * COLS), bf16),
            V((16, 2 * COLS), f32), V((16, 2 * COLS), f32), V((16, 2 * COLS), f32),
            V((VEC, COLS), f32),
            V((24, HALF), f32), V((2, VEC, COLS), f32), V((2, VEC, COLS), f32),
            V((2, 1, 128), f32), V((2, 1, 128), f32),
            D((2, 4)), D((2, 4)), D((2, 16)), D((2, 16)), D((2, 16)), D((2, 16)),
            D((1,)), D((CHIPS,)), D((1,)), D((2 * CHIPS,)), D((5,)), D((5,)), D((2, 16)), D((2, 16)),
            V((FEAT, COLS), f32), V((VEC, COLS), f32), V((VEC, COLS), f32), V((VEC, COLS), f32), D((4,)),
        ],
        compiler_params=pltpu.CompilerParams(
            collective_id=0, has_side_effects=True, vmem_limit_bytes=56 * 2**20
        ),
        name="cg",
    )(points, inv_length, out_scale, noise, solution, residual, direction)
    return out[0:8], out[8:16], out[16:24]


def solution(mesh):
    cols = P(None, ("grp", "mem"))
    return jax.shard_map(
        per_device,
        mesh=mesh,
        in_specs=(cols, P(), P(), P(), cols, cols, cols),
        out_specs=(cols, cols, cols),
        check_vma=False,
    )
```

```python
import math

import jax
import jax.numpy as jnp
from jax import lax
from jax.experimental import pallas as pl
from jax.experimental.pallas import tpu as pltpu
from jax.sharding import PartitionSpec as P

MESH = pl.DeviceIdType.MESH
f32 = jnp.float32
bf16 = jnp.bfloat16

FEAT = 11
VEC = 8
COLS = 256
HALF = 128
CHIPS = 64
GROUPS = 7
LOG2E = math.log2(math.e)
LIFT = 1.5 * LOG2E
SHIFT = 0.75 * LOG2E * LOG2E
SCALE = math.exp(1.5) / (3.0 * LOG2E * LOG2E)


def offsets():
    three = (2, 3, 1)
    out = [(i, j, k) for k in three for j in three for i in three]
    out += [(0, j, k) for k in three for j in three]
    out += [(i, 0, k) for k in three for i in three]
    out += [(i, j, 0) for j in three for i in three]
    out += [(0, 0, k) for k in three] + [(0, j, 0) for j in three] + [(i, 0, 0) for i in three]
    return out


OFFS = offsets()
PLANE = [(1, 1), (3, 3), (1, 3), (3, 1), (2, 1), (1, 2), (2, 3), (3, 2), (2, 2)]


def split3(rows):
    high = rows.astype(bf16)
    rest = rows - high.astype(f32)
    mid = rest.astype(bf16)
    low = (rest - mid.astype(f32)).astype(bf16)
    return high, mid, low


def col_stack(rows):
    h, m, l = split3(rows)
    one = jnp.ones((16, HALF), bf16)
    return jnp.concatenate([h, h, m, m, h, l, one, jnp.zeros_like(one)], 0)


def row_stack(rows, sq):
    h, m, l = split3(rows)
    row = lax.broadcasted_iota(jnp.int32, (16, HALF), 0)
    last = jnp.zeros((16, HALF), f32)
    for n, part in enumerate(split3(sq)):
        last = jnp.where(row == n, part.astype(f32), last)
    return jnp.concatenate([h, m, h, m, l, h, last.astype(bf16), jnp.zeros((16, HALF), bf16)], 0)


def vec_stack(rows):
    high = rows.astype(bf16).astype(f32)
    return jnp.concatenate([high, rows - high], 0).astype(bf16)


def tile_of(t):
    t = jnp.maximum(t, 1e-30)
    w = -LIFT - t * lax.rsqrt(t)
    return (w * w + SHIFT) * jnp.exp2(w)


def mv(x, k):
    return jnp.dot(x, k, preferred_element_type=f32)


def fold(acc):
    return acc[0:VEC] + acc[VEC : 2 * VEC]


def kernel(
    pts_in, inv, scale, noise, sol_in, res_in, dirn_in,
    outs,
    gath, rgath, igath, fgath, isnd, fsnd,
    qtmp, qmat, khi, klo, acc_d, acc_r, acc_i, dots,
    ex_p, ex_s, ex_r, sc_s, sc_r,
    s_blk, r_blk, s_i, r_i, s_f, r_f, s_x, r_x,
    pts, sol, res, dirn, s_in,
):
    g, m = lax.axis_index("grp"), lax.axis_index("mem")
    x, y, z, core = g // 8, (g // 2) % 4, (m // 2) * 2 + g % 2, m % 2
    partner = (g, (m // 2) * 2 + 1 - core)

    def peer(e1, e2, e3, other=0):
        px = (x + e1 + core * (e3 - e1)) % 4
        py = (y + e2) % 4
        pz = (z + e3 + core * (e1 - e3)) % 4
        return ((px * 4 + py) * 2 + pz % 2, (pz // 2) * 2 + (1 - core if other else core))

    loads = (pts_in, pts), (dirn_in, dirn), (res_in, res), (sol_in, sol)
    loads = [pltpu.make_async_copy(a, b, s_in.at[n]) for n, (a, b) in enumerate(loads)]
    for cp in loads:
        cp.start()
    barrier = pltpu.get_barrier_semaphore()

    def greet(device):
        pl.semaphore_signal(barrier, inc=1, device_id=device, device_id_type=MESH)

    greet(partner)
    for e in (1, 3, 2):
        greet(peer(e, 0, 0))
        greet(peer(0, e, 0))
        greet(peer(0, 0, e))
    for e1, e2 in PLANE:
        greet(peer(e1, e2, 0))

    gain = math.sqrt(5.0) * LOG2E
    own, r_own = gath.at[0, 0, 0], rgath.at[0, 0, 0]
    for cp in loads[:2]:
        cp.wait()
    for half, (at, at_sq) in enumerate(((16, 27), (29, 28))):
        lanes = slice(half * HALF, (half + 1) * HALF)
        own[8 * half : 8 * half + 8, :] = dirn[:, lanes]
        sq = jnp.zeros((1, HALF), f32)
        for f in range(FEAT):
            scaled = pts[f : f + 1, lanes] * (inv[f] * gain)
            own[at + f : at + f + 1, :] = scaled
            sq = sq + scaled * scaled
        own[at_sq : at_sq + 1, :] = sq

    def put(src, dst, s, r, device):
        cp = pltpu.make_async_remote_copy(
            src_ref=src, dst_ref=dst, send_sem=s, recv_sem=r, device_id=device, device_id_type=MESH
        )
        cp.start()
        return cp

    def await_(ref, sem):
        pltpu.make_async_copy(ref, ref, sem).wait()

    def exchange(n, src, dst):
        return put(src, dst, s_x.at[n], r_x.at[n], partner)

    bufs = gath, rgath

    def send(w, src, dst, n, device):
        put(bufs[w].at[src], bufs[w].at[dst], s_blk.at[w], r_blk.at[w, n], device)

    def nine(w, n):
        await_(bufs[w].at[pl.ds(0, 3), pl.ds(0, 3), 0], r_blk.at[w, n])

    def leave(w):
        for e in (1, 3, 2):
            send(w, (0, 0, 0), (0, 0, e), 0, peer(e, 0, 0))
            send(w, (0, 0, 0), (0, e, 0), 0, peer(0, e, 0))
        for e in (1, 3, 2):
            send(w, (0, 0, 0), (e, 0, 0), 1, peer(0, 0, e))
        for e1, e2 in PLANE:
            send(w, (0, 0, 0), (0, e2, e1), 2, peer(e1, e2, 0))

    def pass_lines(w):
        await_(bufs[w].at[pl.ds(0, 2), pl.ds(0, 3), 0], r_blk.at[w, 0])
        for f in (1, 3, 2):
            send(w, (0, 0, pl.ds(1, 3)), (f, 0, pl.ds(1, 3)), 3, peer(0, 0, f))
        for f in (1, 3, 2):
            for e in (1, 3, 2):
                send(w, (0, e, 0), (f, e, 0), 4, peer(0, 0, f))
        await_(bufs[w].at[pl.ds(0, 3), 0, 0], r_blk.at[w, 1])

    def pass_plane(w):
        nine(w, 2)
        for f in (1, 3, 2):
            for e in (1, 3, 2):
                send(w, (0, e, pl.ds(2, 2)), (f, e, pl.ds(2, 2)), 4 + f, peer(0, 0, f))

    def pass_second(w):
        nine(w, 3)
        for f in (1, 3, 2):
            for e in (1, 3, 2):
                send(w, (f, 0, 1), (f, e, 1), 4 + f, peer(0, e, 0))

    def rows_side(blk, top, start, n):
        pairs = [(half, cols) for half in (0, 1) for cols in (0, 1)]
        for half, cols in pairs:
            at = (16, 29)[half] - top
            put_at, one_at = ((0, 11), (5, 4))[cols]
            tmp = qtmp.at[n + 2 * half + cols]
            tmp[put_at : put_at + FEAT, :] = -2.0 * blk[at : at + FEAT, :]
            tmp[one_at : one_at + 1, :] = jnp.ones((1, HALF), f32)
        for half, cols in pairs:
            at_sq = (27, 28)[half] - top
            lanes = slice(start + half * HALF, start + (half + 1) * HALF)
            rows = qtmp[n + 2 * half + cols]
            qmat[cols, :, lanes] = row_stack(rows, blk[at_sq : at_sq + 1, :])

    pl.semaphore_wait(barrier, 19)
    cp_p = exchange(0, own.at[pl.ds(16, 24)], ex_p)
    leave(0)
    for acc in (acc_d, acc_r, acc_i, qtmp):
        acc[...] = jnp.zeros_like(acc)
    rows_side(own, 0, 0, 0)
    for cp in loads[2:]:
        cp.wait()
    r_own[...] = res[...]
    cp_p.wait()
    rows_side(ex_p, 16, COLS, 4)

    def build(places):
        for e3, e2, e1 in places:
            k = e3 * 16 + e2 * 4 + e1
            blk = gath.at[e3, e2, e1]
            cols = col_stack(blk[16:32, :]), col_stack(blk[24:40, :])
            vec = vec_stack(blk[0:8, :]), vec_stack(blk[8:16, :])
            for i0 in range(0, 2 * COLS, 256):
                part = acc_d[:, i0 : i0 + 256]
                for half in (0, 1):
                    j0 = half * HALF
                    t = lax.dot_general(
                        cols[half], qmat[half, :, i0 : i0 + 256],
                        (((0,), (0,)), ((), ())), preferred_element_type=f32,
                    )
                    tile = tile_of(t)
                    hi = tile.astype(bf16)
                    lo = (tile - hi.astype(f32)).astype(bf16)
                    khi[k, j0 : j0 + HALF, i0 : i0 + 256] = hi
                    klo[k, j0 : j0 + HALF, i0 : i0 + 256] = lo
                    part = part + mv(vec[half], hi) + mv(vec[half], lo)
                acc_d[:, i0 : i0 + 256] = part

    def times(acc, places, rows_of):
        for i0 in range(0, 2 * COLS, 256):
            part = acc[:, i0 : i0 + 256]
            for e3, e2, e1 in places:
                k = e3 * 16 + e2 * 4 + e1
                v = vec_stack(rows_of(e3, e2, e1))
                part = part + mv(v, khi[k, :, i0 : i0 + 256]) + mv(v, klo[k, :, i0 : i0 + 256])
            acc[:, i0 : i0 + 256] = part

    def pick(grp, *cases):
        out = cases[-1]
        for n in range(len(cases) - 2, -1, -1):
            out = jnp.where(grp == n, cases[n], out)
        return out

    def third(grp):
        return pick(grp, 0, 0, 0, 0, 1, 3, 2)

    def places_of(grp):
        e = third(grp)
        return [
            (
                pick(grp, p if q == 3 else 0, 0, q, q, e),
                pick(grp, p if q == 2 else 0, q, 0, p, q),
                pick(grp, p if q == 1 else 0, p, p, 0, p),
            )
            for q in range(1, 4)
            for p in range(1, 4)
        ]

    build([(0, 0, 0)])
    pass_lines(0)

    @pl.loop(0, GROUPS)
    def _(grp):
        @pl.when(grp == 1)
        def _():
            pass_plane(0)

        @pl.when(grp == 2)
        def _():
            pass_second(0)
            leave(1)

        @pl.when(grp == 3)
        def _():
            nine(0, 4)

        @pl.when(grp >= 4)
        def _():
            nine(0, 4 + third(grp))

        @pl.when(grp == 4)
        def _():
            pass_lines(1)

        @pl.when(grp == 5)
        def _():
            pass_plane(1)

        @pl.when(grp == 6)
        def _():
            pass_second(1)

        build(places_of(grp))

    total = fold(acc_d[...])
    ex_s[0] = total[:, COLS:]
    cp_a = exchange(1, ex_s.at[0], ex_r.at[0])
    times(acc_r, [(0, 0, 0)], lambda e3, e2, e1: rgath[e3, e2, e1])
    cp_a.wait()
    kd = (SCALE * scale[0]) * (total[:, :COLS] + ex_r[0])
    image = kd + noise[0] * dirn[...]
    isnd[...] = image
    igath[0, 0, 0] = image
    for n, (e1, e2, e3) in enumerate(OFFS):
        put(isnd, igath.at[e3, e2, e1], s_i.at[0], r_i.at[n // 9], peer(e1, e2, e3))

    for n in range(4, 8):
        nine(1, n)

    @pl.loop(0, GROUPS)
    def _(grp):
        times(acc_r, places_of(grp), lambda e3, e2, e1: rgath[e3, e2, e1])

    def squares(step):
        def one_step(k, acc):
            v = step(k // 16, (k // 4) % 4, k % 4)
            return acc + v

        return lax.fori_loop(0, CHIPS, one_step, jnp.zeros((VEC, COLS), f32), unroll=8)

    def r_of(e3, e2, e1):
        return rgath[e3, e2, e1]

    rr = squares(lambda *e: r_of(*e) * r_of(*e))
    times(acc_i, [(0, 0, 0)], lambda e3, e2, e1: igath[e3, e2, e1])
    dots[...] = dirn[...] * image

    def meet(places, n):
        di = dots[...]
        await_(igath.at[pl.ds(0, 3), pl.ds(0, 3), 0], r_i.at[n])
        for e3, e2, e1 in places:
            blk = gath.at[e3, e2, e1]
            d = jnp.concatenate([blk[0:8, :], blk[8:16, :]], 1)
            di = di + d * igath[e3, e2, e1]
        dots[...] = di

    @pl.loop(0, GROUPS - 1)
    def _(back):
        places = places_of(GROUPS - 1 - back)
        meet(places, back)
        times(acc_i, places, lambda e3, e2, e1: igath[e3, e2, e1])

    lane = lax.broadcasted_iota(jnp.int32, (VEC, 128), 1)
    sub = lax.broadcasted_iota(jnp.int32, (VEC, 128), 0)

    def pack(*cols):
        out = jnp.zeros((VEC, 128), f32)
        for n, c in enumerate(cols):
            out = jnp.where(lane == n * VEC + sub, c, out)
        return jnp.sum(out, axis=0, keepdims=True)

    def take(a, n):
        return jnp.sum(jnp.where(lane == n * VEC + sub, a, 0.0), axis=1, keepdims=True)

    def total_of(a):
        return jnp.sum(a, axis=1, keepdims=True)

    lines = [(k, 0, 0) for k in (2, 3, 1)] + [(0, j, 0) for j in (2, 3, 1)] + [(0, 0, i) for i in (2, 3, 1)]
    meet(lines, GROUPS - 1)
    mine = pack(total_of(rr), total_of(dots[...]))
    sc_s[0] = mine
    cp_b = exchange(2, sc_s.at[0], sc_r.at[0])
    times(acc_i, lines, lambda e3, e2, e1: igath[e3, e2, e1])
    cp_b.wait()
    both = mine + sc_r[0]
    norm0 = take(both, 0)
    alpha0 = norm0 / take(both, 1)

    def r1_sq(e3, e2, e1):
        r1 = r_of(e3, e2, e1) - alpha0 * igath[e3, e2, e1]
        return r1 * r1

    mine = pack(total_of(squares(r1_sq)))
    sc_s[1] = mine
    cp_c = exchange(3, sc_s.at[1], sc_r.at[1])
    part = fold(acc_r[...]) - alpha0 * fold(acc_i[...])
    ex_s[1] = part[:, COLS:]
    cp_d = exchange(4, ex_s.at[1], ex_r.at[1])
    cp_c.wait()
    norm1 = take(mine + sc_r[1], 0)
    beta = norm1 / norm0
    r1 = res[...] - alpha0 * image
    d1 = r1 + beta * dirn[...]
    cp_d.wait()
    im1 = (SCALE * scale[0]) * (part[:, :COLS] + ex_r[1]) + beta * kd + noise[0] * d1
    mine = pack(total_of(d1 * im1), total_of(r1 * im1), total_of(im1 * im1))
    fsnd[...] = mine
    fgath[0] = mine
    for other in (0, 1):
        for e1, e2, e3 in OFFS + [(0, 0, 0)] * other:
            k = other * CHIPS + e3 * 16 + e2 * 4 + e1
            put(fsnd, fgath.at[k], s_f.at[0], r_f.at[0], peer(e1, e2, e3, other))

    sol1 = sol[...] + alpha0 * dirn[...]
    def others(ref):
        return ref.at[pl.ds(1, 3)], ref.at[0, pl.ds(1, 3)], ref.at[0, 0, pl.ds(1, 3)]

    for w in (0, 1):
        for ref in others(bufs[w]):
            await_(ref, s_blk.at[w])
    for ref in others(igath):
        await_(ref, s_i.at[0])

    await_(fgath.at[pl.ds(1, 2 * CHIPS - 1)], r_f.at[0])
    both = jnp.sum(fgath[...], axis=0)
    alpha1 = norm1 / take(both, 0)
    norm2 = norm1 + alpha1 * (alpha1 * take(both, 2) - 2.0 * take(both, 1))
    r2 = r1 - alpha1 * im1
    outs[0:8, :] = sol1 + alpha1 * d1
    outs[8:16, :] = r2
    outs[16:24, :] = r2 + (norm2 / norm1) * d1
    await_(fgath.at[pl.ds(1, 2 * CHIPS - 1)], s_f.at[0])


def per_device(points, inv_length, out_scale, noise, solution, residual, direction):
    vm = pl.BlockSpec(memory_space=pltpu.VMEM)
    hbm = pl.BlockSpec(memory_space=pl.ANY)
    sm = pl.BlockSpec(memory_space=pltpu.SMEM)
    V, D = pltpu.VMEM, pltpu.SemaphoreType.DMA
    out = pl.pallas_call(
        kernel,
        out_shape=jax.ShapeDtypeStruct((3 * VEC, COLS), f32),
        in_specs=[hbm, sm, sm, sm, hbm, hbm, hbm],
        out_specs=vm,
        scratch_shapes=[
            V((4, 4, 4, 40, HALF), f32), V((4, 4, 4, VEC, COLS), f32), V((4, 4, 4, VEC, COLS), f32),
            V((2 * CHIPS, 1, 128), f32), V((VEC, COLS), f32), V((1, 128), f32),
            V((8, 16, HALF), f32), V((2, 128, 2 * COLS), bf16),
            V((CHIPS, COLS, 2 * COLS), bf16), V((CHIPS, COLS, 2 * COLS), bf16),
            V((16, 2 * COLS), f32), V((16, 2 * COLS), f32), V((16, 2 * COLS), f32),
            V((VEC, COLS), f32),
            V((24, HALF), f32), V((2, VEC, COLS), f32), V((2, VEC, COLS), f32),
            V((2, 1, 128), f32), V((2, 1, 128), f32),
            D((2,)), D((2, 8)), D((1,)), D((GROUPS,)), D((1,)), D((1,)), D((5,)), D((5,)),
            V((FEAT, COLS), f32), V((VEC, COLS), f32), V((VEC, COLS), f32), V((VEC, COLS), f32), D((4,)),
        ],
        compiler_params=pltpu.CompilerParams(
            collective_id=0, has_side_effects=True, vmem_limit_bytes=56 * 2**20
        ),
        name="cg",
    )(points, inv_length, out_scale, noise, solution, residual, direction)
    return out[0:8], out[8:16], out[16:24]


def solution(mesh):
    cols = P(None, ("grp", "mem"))
    return jax.shard_map(
        per_device,
        mesh=mesh,
        in_specs=(cols, P(), P(), P(), cols, cols, cols),
        out_specs=(cols, cols, cols),
        check_vma=False,
    )
```

```python
import math

import jax
import jax.numpy as jnp
from jax import lax
from jax.experimental import pallas as pl
from jax.experimental.pallas import tpu as pltpu
from jax.sharding import PartitionSpec as P

MESH = pl.DeviceIdType.MESH
f32 = jnp.float32
bf16 = jnp.bfloat16

FEAT = 11
VEC = 8
COLS = 256
HALF = 128
CHIPS = 64
GROUPS = 7
LOG2E = math.log2(math.e)
LIFT = 1.5 * LOG2E
SHIFT = 0.75 * LOG2E * LOG2E
SCALE = math.exp(1.5) / (3.0 * LOG2E * LOG2E)


def offsets():
    three = (2, 3, 1)
    out = [(i, j, k) for k in three for j in three for i in three]
    out += [(0, j, k) for k in three for j in three]
    out += [(i, 0, k) for k in three for i in three]
    out += [(i, j, 0) for j in three for i in three]
    out += [(0, 0, k) for k in three] + [(0, j, 0) for j in three] + [(i, 0, 0) for i in three]
    return out


OFFS = offsets()
PLANE = [(1, 1), (3, 3), (1, 3), (3, 1), (2, 1), (1, 2), (2, 3), (3, 2), (2, 2)]


def split3(rows):
    high = rows.astype(bf16)
    rest = rows - high.astype(f32)
    mid = rest.astype(bf16)
    low = (rest - mid.astype(f32)).astype(bf16)
    return high, mid, low


def col_stack(rows):
    h, m, l = split3(rows)
    one = jnp.ones((16, HALF), bf16)
    return jnp.concatenate([h, h, m, m, h, l, one, jnp.zeros_like(one)], 0)


def row_stack(rows, sq):
    h, m, l = split3(rows)
    row = lax.broadcasted_iota(jnp.int32, (16, HALF), 0)
    last = jnp.zeros((16, HALF), f32)
    for n, part in enumerate(split3(sq)):
        last = jnp.where(row == n, part.astype(f32), last)
    return jnp.concatenate([h, m, h, m, l, h, last.astype(bf16), jnp.zeros((16, HALF), bf16)], 0)


def vec_stack(rows):
    high = rows.astype(bf16).astype(f32)
    return jnp.concatenate([high, rows - high], 0).astype(bf16)


def tile_of(t):
    t = jnp.maximum(t, 1e-30)
    w = -LIFT - t * lax.rsqrt(t)
    return (w * w + SHIFT) * jnp.exp2(w)


def mv(x, k):
    return jnp.dot(x, k, preferred_element_type=f32)


def fold(acc):
    return acc[0:VEC] + acc[VEC : 2 * VEC]


def kernel(
    pts_in, inv, scale, noise, sol_in, res_in, dirn_in,
    outs,
    gath, rgath, igath, fgath, isnd, fsnd,
    qtmp, qmat, khi, klo, acc_d, acc_r, acc_i,
    ex_p, ex_s, ex_r, sc_s, sc_r,
    s_blk, r_blk, s_i, r_i, s_f, r_f, s_x, r_x,
    pts, sol, res, dirn, s_in,
):
    g, m = lax.axis_index("grp"), lax.axis_index("mem")
    x, y, z, core = g // 8, (g // 2) % 4, (m // 2) * 2 + g % 2, m % 2
    partner = (g, (m // 2) * 2 + 1 - core)

    def peer(e1, e2, e3, other=0):
        px = (x + e1 + core * (e3 - e1)) % 4
        py = (y + e2) % 4
        pz = (z + e3 + core * (e1 - e3)) % 4
        return ((px * 4 + py) * 2 + pz % 2, (pz // 2) * 2 + (1 - core if other else core))

    loads = (pts_in, pts), (dirn_in, dirn), (res_in, res), (sol_in, sol)
    loads = [pltpu.make_async_copy(a, b, s_in.at[n]) for n, (a, b) in enumerate(loads)]
    for cp in loads:
        cp.start()
    barrier = pltpu.get_barrier_semaphore()

    def greet(device):
        pl.semaphore_signal(barrier, inc=1, device_id=device, device_id_type=MESH)

    greet(partner)
    for e in (1, 3, 2):
        greet(peer(e, 0, 0))
        greet(peer(0, e, 0))
        greet(peer(0, 0, e))
    for e1, e2 in PLANE:
        greet(peer(e1, e2, 0))

    gain = math.sqrt(5.0) * LOG2E
    own, r_own = gath.at[0, 0, 0], rgath.at[0, 0, 0]
    for cp in loads[:2]:
        cp.wait()
    for half, (at, at_sq) in enumerate(((16, 27), (29, 28))):
        lanes = slice(half * HALF, (half + 1) * HALF)
        own[8 * half : 8 * half + 8, :] = dirn[:, lanes]
        sq = jnp.zeros((1, HALF), f32)
        for f in range(FEAT):
            scaled = pts[f : f + 1, lanes] * (inv[f] * gain)
            own[at + f : at + f + 1, :] = scaled
            sq = sq + scaled * scaled
        own[at_sq : at_sq + 1, :] = sq

    def put(src, dst, s, r, device):
        cp = pltpu.make_async_remote_copy(
            src_ref=src, dst_ref=dst, send_sem=s, recv_sem=r, device_id=device, device_id_type=MESH
        )
        cp.start()
        return cp

    def await_(ref, sem):
        pltpu.make_async_copy(ref, ref, sem).wait()

    def exchange(n, src, dst):
        return put(src, dst, s_x.at[n], r_x.at[n], partner)

    bufs = gath, rgath

    def send(w, src, dst, n, device):
        put(bufs[w].at[src], bufs[w].at[dst], s_blk.at[w], r_blk.at[w, n], device)

    def nine(w, n):
        await_(bufs[w].at[pl.ds(0, 3), pl.ds(0, 3), 0], r_blk.at[w, n])

    def leave(w):
        for e in (1, 3, 2):
            send(w, (0, 0, 0), (0, 0, e), 0, peer(e, 0, 0))
            send(w, (0, 0, 0), (0, e, 0), 0, peer(0, e, 0))
        for e in (1, 3, 2):
            send(w, (0, 0, 0), (e, 0, 0), 1, peer(0, 0, e))
        for e1, e2 in PLANE:
            send(w, (0, 0, 0), (0, e2, e1), 2, peer(e1, e2, 0))

    def pass_lines(w):
        await_(bufs[w].at[pl.ds(0, 2), pl.ds(0, 3), 0], r_blk.at[w, 0])
        for f in (1, 3, 2):
            send(w, (0, 0, pl.ds(1, 3)), (f, 0, pl.ds(1, 3)), 3, peer(0, 0, f))
        for f in (1, 3, 2):
            for e in (1, 3, 2):
                send(w, (0, e, 0), (f, e, 0), 4, peer(0, 0, f))
        await_(bufs[w].at[pl.ds(0, 3), 0, 0], r_blk.at[w, 1])

    def pass_plane(w):
        nine(w, 2)
        for f in (1, 3, 2):
            for e in (1, 3, 2):
                send(w, (0, e, pl.ds(2, 2)), (f, e, pl.ds(2, 2)), 4 + f, peer(0, 0, f))

    def pass_second(w):
        nine(w, 3)
        for f in (1, 3, 2):
            for e in (1, 3, 2):
                send(w, (f, 0, 1), (f, e, 1), 4 + f, peer(0, e, 0))

    def rows_side(blk, top, start, n):
        pairs = [(half, cols) for half in (0, 1) for cols in (0, 1)]
        for half, cols in pairs:
            at = (16, 29)[half] - top
            put_at, one_at = ((0, 11), (5, 4))[cols]
            tmp = qtmp.at[n + 2 * half + cols]
            tmp[put_at : put_at + FEAT, :] = -2.0 * blk[at : at + FEAT, :]
            tmp[one_at : one_at + 1, :] = jnp.ones((1, HALF), f32)
        for half, cols in pairs:
            at_sq = (27, 28)[half] - top
            lanes = slice(start + half * HALF, start + (half + 1) * HALF)
            rows = qtmp[n + 2 * half + cols]
            qmat[cols, :, lanes] = row_stack(rows, blk[at_sq : at_sq + 1, :])

    pl.semaphore_wait(barrier, 19)
    cp_p = exchange(0, own.at[pl.ds(16, 24)], ex_p)
    leave(0)
    for acc in (acc_d, acc_r, acc_i, qtmp):
        acc[...] = jnp.zeros_like(acc)
    rows_side(own, 0, 0, 0)
    for cp in loads[2:]:
        cp.wait()
    r_own[...] = res[...]
    cp_p.wait()
    rows_side(ex_p, 16, COLS, 4)

    def build(places, starts=(0, 256)):
        for e3, e2, e1 in places:
            k = e3 * 16 + e2 * 4 + e1
            blk = gath.at[e3, e2, e1]
            cols = col_stack(blk[16:32, :]), col_stack(blk[24:40, :])
            vec = vec_stack(blk[0:8, :]), vec_stack(blk[8:16, :])
            for i0 in starts:
                part = acc_d[:, i0 : i0 + 256]
                for half in (0, 1):
                    j0 = half * HALF
                    t = lax.dot_general(
                        cols[half], qmat[half, :, i0 : i0 + 256],
                        (((0,), (0,)), ((), ())), preferred_element_type=f32,
                    )
                    tile = tile_of(t)
                    hi = tile.astype(bf16)
                    lo = (tile - hi.astype(f32)).astype(bf16)
                    khi[k, j0 : j0 + HALF, i0 : i0 + 256] = hi
                    klo[k, j0 : j0 + HALF, i0 : i0 + 256] = lo
                    part = part + mv(vec[half], hi) + mv(vec[half], lo)
                acc_d[:, i0 : i0 + 256] = part

    def times(acc, places, rows_of, starts=(0, 256)):
        for i0 in starts:
            part = acc[:, i0 : i0 + 256]
            for e3, e2, e1 in places:
                k = e3 * 16 + e2 * 4 + e1
                v = vec_stack(rows_of(e3, e2, e1))
                part = part + mv(v, khi[k, :, i0 : i0 + 256]) + mv(v, klo[k, :, i0 : i0 + 256])
            acc[:, i0 : i0 + 256] = part

    def pick(grp, *cases):
        out = cases[-1]
        for n in range(len(cases) - 2, -1, -1):
            out = jnp.where(grp == n, cases[n], out)
        return out

    def third(grp):
        return pick(grp, 0, 0, 0, 0, 1, 3, 2)

    def places_of(grp):
        e = third(grp)
        return [
            (
                pick(grp, p if q == 3 else 0, 0, q, q, e),
                pick(grp, p if q == 2 else 0, q, 0, p, q),
                pick(grp, p if q == 1 else 0, p, p, 0, p),
            )
            for q in range(1, 4)
            for p in range(1, 4)
        ]

    build([(0, 0, 0)])
    pass_lines(0)

    @pl.loop(0, GROUPS - 1)
    def _(grp):
        @pl.when(grp == 1)
        def _():
            pass_plane(0)

        @pl.when(grp == 2)
        def _():
            pass_second(0)
            leave(1)

        @pl.when(grp == 3)
        def _():
            nine(0, 4)

        @pl.when(grp >= 4)
        def _():
            nine(0, 4 + third(grp))

        @pl.when(grp == 4)
        def _():
            pass_lines(1)

        @pl.when(grp == 5)
        def _():
            pass_plane(1)

        build(places_of(grp))

    last = [(2, j, i) for j in range(1, 4) for i in range(1, 4)]
    nine(0, 6)
    pass_second(1)
    build(last, (256,))
    ex_s[0] = fold(acc_d[:, COLS:])
    cp_a = exchange(1, ex_s.at[0], ex_r.at[0])
    build(last, (0,))
    total = fold(acc_d[:, :COLS])
    cp_a.wait()

    kd = (SCALE * scale[0]) * (total + ex_r[0])
    image = kd + noise[0] * dirn[...]
    isnd[...] = image
    igath[0, 0, 0] = image
    for n, (e1, e2, e3) in enumerate(OFFS):
        put(isnd, igath.at[e3, e2, e1], s_i.at[0], r_i.at[n // 9], peer(e1, e2, e3))

    lane = lax.broadcasted_iota(jnp.int32, (VEC, 128), 1)
    sub = lax.broadcasted_iota(jnp.int32, (VEC, 128), 0)

    def pack(*cols):
        out = jnp.zeros((VEC, 128), f32)
        for n, c in enumerate(cols):
            out = jnp.where(lane == n * VEC + sub, c, out)
        return jnp.sum(out, axis=0, keepdims=True)

    def take(a, n):
        return jnp.sum(jnp.where(lane == n * VEC + sub, a, 0.0), axis=1, keepdims=True)

    def total_of(a):
        return jnp.sum(a, axis=1, keepdims=True)

    def tell(row, src, dst, s, r):
        src[...] = row
        dst[0] = row
        for other in (0, 1):
            for e1, e2, e3 in OFFS + [(0, 0, 0)] * other:
                k = other * CHIPS + e3 * 16 + e2 * 4 + e1
                put(src, dst.at[k], s.at[0], r.at[0], peer(e1, e2, e3, other))

    def told(dst, r):
        await_(dst.at[pl.ds(1, 2 * CHIPS - 1)], r.at[0])
        return jnp.sum(dst[...], axis=0)


    times(acc_r, [(0, 0, 0)], lambda e3, e2, e1: rgath[e3, e2, e1])
    for n in range(4, 8):
        nine(1, n)

    @pl.loop(0, GROUPS)
    def _(grp):
        times(acc_r, places_of(grp), lambda e3, e2, e1: rgath[e3, e2, e1])

    def image_of(e3, e2, e1):
        return igath[e3, e2, e1]

    def met(n):
        await_(igath.at[pl.ds(0, 3), pl.ds(0, 3), 0], r_i.at[n])

    times(acc_i, [(0, 0, 0)], image_of)

    def sums(acc, places):
        rr, di = acc
        for e3, e2, e1 in places:
            blk, r = gath.at[e3, e2, e1], rgath[e3, e2, e1]
            d = jnp.concatenate([blk[0:8, :], blk[8:16, :]], 1)
            rr = rr + r * r
            di = di + d * igath[e3, e2, e1]
        return rr, di

    def r1_sq(acc, places):
        for e3, e2, e1 in places:
            v = rgath[e3, e2, e1] - alpha0 * igath[e3, e2, e1]
            acc = acc + v * v
        return acc

    EARLY = 4

    @pl.loop(0, EARLY)
    def _(back):
        met(back)
        times(acc_i, places_of(GROUPS - 1 - back), image_of)

    late = [
        [(j, 0, i) for j in range(1, 4) for i in range(1, 4)],
        [(0, j, i) for j in range(1, 4) for i in range(1, 4)],
        [(k, 0, 0) for k in (2, 3, 1)] + [(0, j, 0) for j in (2, 3, 1)] + [(0, 0, i) for i in (2, 3, 1)],
    ]
    zero = jnp.zeros((VEC, COLS), f32)
    full = [(j, i) for j in range(4) for i in range(4)]
    deep = [(j, i) for j in range(1, 4) for i in range(4)]
    acc = lax.fori_loop(1, 4, lambda k, acc: sums(acc, [(k, j, i) for j, i in deep]), (zero, zero))
    acc = sums(acc, [(0, 0, 0)])
    for n, places in enumerate(late):
        met(EARLY + n)
        acc = sums(acc, places)
    mine = pack(total_of(acc[0]), total_of(acc[1]))
    sc_s[0] = mine
    cp_b = exchange(2, sc_s.at[0], sc_r.at[0])
    times(acc_i, late[0] + late[1], image_of)
    cp_b.wait()
    both = mine + sc_r[0]
    norm0 = take(both, 0)
    alpha0 = norm0 / take(both, 1)
    acc = lax.fori_loop(0, 4, lambda k, acc: r1_sq(acc, [(k, j, i) for j, i in full]), zero)
    mine = pack(total_of(acc))
    sc_s[1] = mine
    cp_c = exchange(3, sc_s.at[1], sc_r.at[1])
    times(acc_i, late[2], image_of, (256,))
    ex_s[1] = fold(acc_r[:, COLS:]) - alpha0 * fold(acc_i[:, COLS:])
    cp_d = exchange(4, ex_s.at[1], ex_r.at[1])
    times(acc_i, late[2], image_of, (0,))
    part = fold(acc_r[:, :COLS]) - alpha0 * fold(acc_i[:, :COLS])
    r1 = res[...] - alpha0 * image
    cp_c.wait()
    norm1 = take(mine + sc_r[1], 0)
    beta = norm1 / norm0
    d1 = r1 + beta * dirn[...]
    cp_d.wait()
    im1 = (SCALE * scale[0]) * (part + ex_r[1]) + beta * kd + noise[0] * d1
    tell(pack(total_of(d1 * im1), total_of(r1 * im1), total_of(im1 * im1)), fsnd, fgath, s_f, r_f)

    sol1 = sol[...] + alpha0 * dirn[...]
    def others(ref):
        return ref.at[pl.ds(1, 3)], ref.at[0, pl.ds(1, 3)], ref.at[0, 0, pl.ds(1, 3)]

    for w in (0, 1):
        for ref in others(bufs[w]):
            await_(ref, s_blk.at[w])
    for ref in others(igath):
        await_(ref, s_i.at[0])


    both = told(fgath, r_f)
    alpha1 = norm1 / take(both, 0)
    norm2 = norm1 + alpha1 * (alpha1 * take(both, 2) - 2.0 * take(both, 1))
    r2 = r1 - alpha1 * im1
    outs[0:8, :] = sol1 + alpha1 * d1
    outs[8:16, :] = r2
    outs[16:24, :] = r2 + (norm2 / norm1) * d1
    await_(fgath.at[pl.ds(1, 2 * CHIPS - 1)], s_f.at[0])


def per_device(points, inv_length, out_scale, noise, solution, residual, direction):
    vm = pl.BlockSpec(memory_space=pltpu.VMEM)
    hbm = pl.BlockSpec(memory_space=pl.ANY)
    sm = pl.BlockSpec(memory_space=pltpu.SMEM)
    V, D = pltpu.VMEM, pltpu.SemaphoreType.DMA
    out = pl.pallas_call(
        kernel,
        out_shape=jax.ShapeDtypeStruct((3 * VEC, COLS), f32),
        in_specs=[hbm, sm, sm, sm, hbm, hbm, hbm],
        out_specs=vm,
        scratch_shapes=[
            V((4, 4, 4, 40, HALF), f32), V((4, 4, 4, VEC, COLS), f32), V((4, 4, 4, VEC, COLS), f32),
            V((2 * CHIPS, 1, 128), f32), V((VEC, COLS), f32), V((1, 128), f32),
            V((8, 16, HALF), f32), V((2, 128, 2 * COLS), bf16),
            V((CHIPS, COLS, 2 * COLS), bf16), V((CHIPS, COLS, 2 * COLS), bf16),
            V((16, 2 * COLS), f32), V((16, 2 * COLS), f32), V((16, 2 * COLS), f32),
            V((24, HALF), f32), V((2, VEC, COLS), f32), V((2, VEC, COLS), f32),
            V((2, 1, 128), f32), V((2, 1, 128), f32),
            D((2,)), D((2, 8)), D((1,)), D((GROUPS,)), D((1,)), D((1,)), D((5,)), D((5,)),
            V((FEAT, COLS), f32), V((VEC, COLS), f32), V((VEC, COLS), f32), V((VEC, COLS), f32), D((4,)),
        ],
        compiler_params=pltpu.CompilerParams(
            collective_id=0, has_side_effects=True, vmem_limit_bytes=56 * 2**20
        ),
        name="cg",
    )(points, inv_length, out_scale, noise, solution, residual, direction)
    return out[0:8], out[8:16], out[16:24]


def solution(mesh):
    cols = P(None, ("grp", "mem"))
    return jax.shard_map(
        per_device,
        mesh=mesh,
        in_specs=(cols, P(), P(), P(), cols, cols, cols),
        out_specs=(cols, cols, cols),
        check_vma=False,
    )
```

```python
import math

import jax
import jax.numpy as jnp
from jax import lax
from jax.experimental import pallas as pl
from jax.experimental.pallas import tpu as pltpu
from jax.sharding import PartitionSpec as P

MESH = pl.DeviceIdType.MESH
f32 = jnp.float32
bf16 = jnp.bfloat16

FEAT = 11
VEC = 8
COLS = 256
HALF = 128
CHIPS = 64
GROUPS = 7
LOG2E = math.log2(math.e)
LIFT = 1.5 * LOG2E
SHIFT = 0.75 * LOG2E * LOG2E
SCALE = math.exp(1.5) / (3.0 * LOG2E * LOG2E)


def offsets():
    three = (2, 3, 1)
    out = [(i, j, k) for k in three for j in three for i in three]
    out += [(0, j, k) for k in three for j in three]
    out += [(i, 0, k) for k in three for i in three]
    out += [(i, j, 0) for j in three for i in three]
    out += [(0, 0, k) for k in three] + [(0, j, 0) for j in three] + [(i, 0, 0) for i in three]
    return out


OFFS = offsets()


def hops(off):
    return sum((0, 1, 2, 1)[d] for d in off)


PLANE = [(1, 1), (3, 3), (1, 3), (3, 1), (2, 1), (1, 2), (2, 3), (3, 2), (2, 2)]


def split3(rows):
    high = rows.astype(bf16)
    rest = rows - high.astype(f32)
    mid = rest.astype(bf16)
    low = (rest - mid.astype(f32)).astype(bf16)
    return high, mid, low


def col_stack(rows):
    h, m, l = split3(rows)
    one = jnp.ones((16, HALF), bf16)
    return jnp.concatenate([h, h, m, m, h, l, one, jnp.zeros_like(one)], 0)


def row_stack(rows, sq):
    h, m, l = split3(rows)
    row = lax.broadcasted_iota(jnp.int32, (16, HALF), 0)
    last = jnp.zeros((16, HALF), f32)
    for n, part in enumerate(split3(sq)):
        last = jnp.where(row == n, part.astype(f32), last)
    return jnp.concatenate([h, m, h, m, l, h, last.astype(bf16), jnp.zeros((16, HALF), bf16)], 0)


def vec_stack(rows):
    high = rows.astype(bf16).astype(f32)
    return jnp.concatenate([high, rows - high], 0).astype(bf16)


def tile_of(t):
    t = jnp.maximum(t, 1e-30)
    w = -LIFT - t * lax.rsqrt(t)
    return (w * w + SHIFT) * jnp.exp2(w)


def mv(x, k):
    return jnp.dot(x, k, preferred_element_type=f32)


def fold(acc):
    return acc[0:VEC] + acc[VEC : 2 * VEC]


def kernel(
    pts_in, inv, scale, noise, sol_in, res_in, dirn_in,
    outs,
    gath, rgath, igath, fgath, isnd, fsnd,
    qtmp, qmat, khi, klo, acc_d, acc_r, acc_i,
    ex_p, ex_s, ex_r, sc_s, sc_r,
    s_blk, r_blk, s_i, r_i, s_f, r_f, s_x, r_x,
    pts, sol, res, dirn, s_in,
):
    g, m = lax.axis_index("grp"), lax.axis_index("mem")
    x, y, z, core = g // 8, (g // 2) % 4, (m // 2) * 2 + g % 2, m % 2
    partner = (g, (m // 2) * 2 + 1 - core)

    def peer(e1, e2, e3, other=0):
        px = (x + e1 + core * (e3 - e1)) % 4
        py = (y + e2) % 4
        pz = (z + e3 + core * (e1 - e3)) % 4
        return ((px * 4 + py) * 2 + pz % 2, (pz // 2) * 2 + (1 - core if other else core))

    loads = (pts_in, pts), (dirn_in, dirn), (res_in, res), (sol_in, sol)
    loads = [pltpu.make_async_copy(a, b, s_in.at[n]) for n, (a, b) in enumerate(loads)]
    for cp in loads:
        cp.start()
    barrier = pltpu.get_barrier_semaphore()

    def greet(device):
        pl.semaphore_signal(barrier, inc=1, device_id=device, device_id_type=MESH)

    greet(partner)
    for e in (1, 3, 2):
        greet(peer(e, 0, 0))
        greet(peer(0, e, 0))
        greet(peer(0, 0, e))
    for e1, e2 in PLANE:
        greet(peer(e1, e2, 0))

    gain = math.sqrt(5.0) * LOG2E
    own, r_own = gath.at[0, 0, 0], rgath.at[0, 0, 0]
    for cp in loads[:2]:
        cp.wait()
    for half, (at, at_sq) in enumerate(((16, 27), (29, 28))):
        lanes = slice(half * HALF, (half + 1) * HALF)
        own[8 * half : 8 * half + 8, :] = dirn[:, lanes]
        sq = jnp.zeros((1, HALF), f32)
        for f in range(FEAT):
            scaled = pts[f : f + 1, lanes] * (inv[f] * gain)
            own[at + f : at + f + 1, :] = scaled
            sq = sq + scaled * scaled
        own[at_sq : at_sq + 1, :] = sq

    def put(src, dst, s, r, device):
        cp = pltpu.make_async_remote_copy(
            src_ref=src, dst_ref=dst, send_sem=s, recv_sem=r, device_id=device, device_id_type=MESH
        )
        cp.start()
        return cp

    def await_(ref, sem):
        pltpu.make_async_copy(ref, ref, sem).wait()

    def exchange(n, src, dst):
        return put(src, dst, s_x.at[n], r_x.at[n], partner)

    bufs = gath, rgath

    def send(w, src, dst, n, device):
        put(bufs[w].at[src], bufs[w].at[dst], s_blk.at[w], r_blk.at[w, n], device)

    def nine(w, n):
        await_(bufs[w].at[pl.ds(0, 3), pl.ds(0, 3), 0], r_blk.at[w, n])

    def leave(w):
        for e in (1, 3, 2):
            send(w, (0, 0, 0), (0, 0, e), 0, peer(e, 0, 0))
            send(w, (0, 0, 0), (0, e, 0), 0, peer(0, e, 0))
        for e in (1, 3, 2):
            send(w, (0, 0, 0), (e, 0, 0), 1, peer(0, 0, e))
        for e1, e2 in PLANE:
            send(w, (0, 0, 0), (0, e2, e1), 2, peer(e1, e2, 0))

    def pass_lines(w):
        await_(bufs[w].at[pl.ds(0, 2), pl.ds(0, 3), 0], r_blk.at[w, 0])
        for f in (1, 3, 2):
            send(w, (0, 0, pl.ds(1, 3)), (f, 0, pl.ds(1, 3)), 3, peer(0, 0, f))
        for f in (1, 3, 2):
            for e in (1, 3, 2):
                send(w, (0, e, 0), (f, e, 0), 4, peer(0, 0, f))
        await_(bufs[w].at[pl.ds(0, 3), 0, 0], r_blk.at[w, 1])

    def pass_plane(w):
        nine(w, 2)
        for f in (1, 3, 2):
            for e in (1, 3, 2):
                send(w, (0, e, pl.ds(1, 3)), (f, e, pl.ds(1, 3)), 4 + f, peer(0, 0, f))

    def rows_side(blk, top, start, n):
        pairs = [(half, cols) for half in (0, 1) for cols in (0, 1)]
        for half, cols in pairs:
            at = (16, 29)[half] - top
            put_at, one_at = ((0, 11), (5, 4))[cols]
            tmp = qtmp.at[n + 2 * half + cols]
            tmp[put_at : put_at + FEAT, :] = -2.0 * blk[at : at + FEAT, :]
            tmp[one_at : one_at + 1, :] = jnp.ones((1, HALF), f32)
        for half, cols in pairs:
            at_sq = (27, 28)[half] - top
            lanes = slice(start + half * HALF, start + (half + 1) * HALF)
            rows = qtmp[n + 2 * half + cols]
            qmat[cols, :, lanes] = row_stack(rows, blk[at_sq : at_sq + 1, :])

    pl.semaphore_wait(barrier, 19)
    cp_p = exchange(0, own.at[pl.ds(16, 24)], ex_p)
    leave(0)
    for acc in (acc_d, acc_r, acc_i, qtmp):
        acc[...] = jnp.zeros_like(acc)
    rows_side(own, 0, 0, 0)
    for cp in loads[2:]:
        cp.wait()
    r_own[...] = res[...]
    cp_p.wait()
    rows_side(ex_p, 16, COLS, 4)

    def build(places, starts=(0, 256)):
        for e3, e2, e1 in places:
            k = e3 * 16 + e2 * 4 + e1
            blk = gath.at[e3, e2, e1]
            cols = col_stack(blk[16:32, :]), col_stack(blk[24:40, :])
            vec = vec_stack(blk[0:8, :]), vec_stack(blk[8:16, :])
            for i0 in starts:
                part = acc_d[:, i0 : i0 + 256]
                for half in (0, 1):
                    j0 = half * HALF
                    t = lax.dot_general(
                        cols[half], qmat[half, :, i0 : i0 + 256],
                        (((0,), (0,)), ((), ())), preferred_element_type=f32,
                    )
                    tile = tile_of(t)
                    hi = tile.astype(bf16)
                    lo = (tile - hi.astype(f32)).astype(bf16)
                    khi[k, j0 : j0 + HALF, i0 : i0 + 256] = hi
                    klo[k, j0 : j0 + HALF, i0 : i0 + 256] = lo
                    part = part + mv(vec[half], hi) + mv(vec[half], lo)
                acc_d[:, i0 : i0 + 256] = part

    def times(acc, places, rows_of, starts=(0, 256)):
        for i0 in starts:
            part = acc[:, i0 : i0 + 256]
            for e3, e2, e1 in places:
                k = e3 * 16 + e2 * 4 + e1
                v = vec_stack(rows_of(e3, e2, e1))
                part = part + mv(v, khi[k, :, i0 : i0 + 256]) + mv(v, klo[k, :, i0 : i0 + 256])
            acc[:, i0 : i0 + 256] = part

    def pick(grp, *cases):
        out = cases[-1]
        for n in range(len(cases) - 2, -1, -1):
            out = jnp.where(grp == n, cases[n], out)
        return out

    def third(grp):
        return pick(grp, 0, 0, 0, 0, 1, 3, 2)

    def places_of(grp):
        e = third(grp)
        return [
            (
                pick(grp, p if q == 3 else 0, 0, q, q, e),
                pick(grp, p if q == 2 else 0, q, 0, p, q),
                pick(grp, p if q == 1 else 0, p, p, 0, p),
            )
            for q in range(1, 4)
            for p in range(1, 4)
        ]

    build([(0, 0, 0)])
    pass_lines(0)

    @pl.loop(0, GROUPS - 1)
    def _(grp):
        @pl.when(grp == 1)
        def _():
            pass_plane(0)

        @pl.when(grp == 2)
        def _():
            nine(0, 3)

        @pl.when(grp == 3)
        def _():
            nine(0, 4)
            leave(1)

        @pl.when(grp >= 4)
        def _():
            nine(0, 4 + third(grp))

        @pl.when(grp == 5)
        def _():
            pass_lines(1)

        build(places_of(grp))

    last = [(2, j, i) for j in range(1, 4) for i in range(1, 4)]
    nine(0, 6)
    pass_plane(1)
    build(last, (256,))
    ex_s[0] = fold(acc_d[:, COLS:])
    cp_a = exchange(1, ex_s.at[0], ex_r.at[0])
    build(last, (0,))
    total = fold(acc_d[:, :COLS])
    cp_a.wait()

    kd = (SCALE * scale[0]) * (total + ex_r[0])
    image = kd + noise[0] * dirn[...]
    isnd[...] = image
    igath[0, 0, 0] = image
    for n, (e1, e2, e3) in enumerate(OFFS):
        put(isnd, igath.at[e3, e2, e1], s_i.at[0], r_i.at[n // 9], peer(e1, e2, e3))

    lane = lax.broadcasted_iota(jnp.int32, (VEC, 128), 1)
    sub = lax.broadcasted_iota(jnp.int32, (VEC, 128), 0)

    def pack(*cols):
        out = jnp.zeros((VEC, 128), f32)
        for n, c in enumerate(cols):
            out = jnp.where(lane == n * VEC + sub, c, out)
        return jnp.sum(out, axis=0, keepdims=True)

    def take(a, n):
        return jnp.sum(jnp.where(lane == n * VEC + sub, a, 0.0), axis=1, keepdims=True)

    def total_of(a):
        return jnp.sum(a, axis=1, keepdims=True)

    def tell(row, src, dst, s, r):
        src[...] = row
        dst[0] = row
        every = [(e, other) for other in (0, 1) for e in OFFS + [(0, 0, 0)] * other]
        for (e1, e2, e3), other in sorted(every, key=lambda e: -hops(e[0])):
            k = other * CHIPS + e3 * 16 + e2 * 4 + e1
            put(src, dst.at[k], s.at[0], r.at[0], peer(e1, e2, e3, other))

    def told(dst, r):
        await_(dst.at[pl.ds(1, 2 * CHIPS - 1)], r.at[0])
        return jnp.sum(dst[...], axis=0)


    times(acc_r, [(0, 0, 0)], lambda e3, e2, e1: rgath[e3, e2, e1])
    nine(1, 3)

    @pl.loop(0, GROUPS)
    def _(grp):
        @pl.when(grp == 3)
        def _():
            nine(1, 4)

        @pl.when(grp >= 4)
        def _():
            nine(1, 4 + third(grp))

        times(acc_r, places_of(grp), lambda e3, e2, e1: rgath[e3, e2, e1])

    def image_of(e3, e2, e1):
        return igath[e3, e2, e1]

    def met(n):
        await_(igath.at[pl.ds(0, 3), pl.ds(0, 3), 0], r_i.at[n])

    times(acc_i, [(0, 0, 0)], image_of)

    def sums(acc, places):
        rr, di = acc
        for e3, e2, e1 in places:
            blk, r = gath.at[e3, e2, e1], rgath[e3, e2, e1]
            d = jnp.concatenate([blk[0:8, :], blk[8:16, :]], 1)
            rr = rr + r * r
            di = di + d * igath[e3, e2, e1]
        return rr, di

    def r1_sq(acc, places):
        for e3, e2, e1 in places:
            v = rgath[e3, e2, e1] - alpha0 * igath[e3, e2, e1]
            acc = acc + v * v
        return acc

    EARLY = 4

    @pl.loop(0, EARLY)
    def _(back):
        met(back)
        times(acc_i, places_of(GROUPS - 1 - back), image_of)

    late = [
        [(j, 0, i) for j in range(1, 4) for i in range(1, 4)],
        [(0, j, i) for j in range(1, 4) for i in range(1, 4)],
        [(k, 0, 0) for k in (2, 3, 1)] + [(0, j, 0) for j in (2, 3, 1)] + [(0, 0, i) for i in (2, 3, 1)],
    ]
    zero = jnp.zeros((VEC, COLS), f32)
    full = [(j, i) for j in range(4) for i in range(4)]
    deep = [(j, i) for j in range(1, 4) for i in range(4)]
    acc = lax.fori_loop(1, 4, lambda k, acc: sums(acc, [(k, j, i) for j, i in deep]), (zero, zero))
    acc = sums(acc, [(0, 0, 0)])
    for n, places in enumerate(late):
        met(EARLY + n)
        acc = sums(acc, places)
    mine = pack(total_of(acc[0]), total_of(acc[1]))
    sc_s[0] = mine
    cp_b = exchange(2, sc_s.at[0], sc_r.at[0])
    times(acc_i, late[0] + late[1], image_of)
    cp_b.wait()
    both = mine + sc_r[0]
    norm0 = take(both, 0)
    alpha0 = norm0 / take(both, 1)
    acc = lax.fori_loop(0, 4, lambda k, acc: r1_sq(acc, [(k, j, i) for j, i in full]), zero)
    mine = pack(total_of(acc))
    sc_s[1] = mine
    cp_c = exchange(3, sc_s.at[1], sc_r.at[1])
    times(acc_i, late[2], image_of, (256,))
    ex_s[1] = fold(acc_r[:, COLS:]) - alpha0 * fold(acc_i[:, COLS:])
    cp_d = exchange(4, ex_s.at[1], ex_r.at[1])
    times(acc_i, late[2], image_of, (0,))
    part = fold(acc_r[:, :COLS]) - alpha0 * fold(acc_i[:, :COLS])
    r1 = res[...] - alpha0 * image
    cp_c.wait()
    norm1 = take(mine + sc_r[1], 0)
    beta = norm1 / norm0
    d1 = r1 + beta * dirn[...]
    cp_d.wait()
    im1 = (SCALE * scale[0]) * (part + ex_r[1]) + beta * kd + noise[0] * d1
    tell(pack(total_of(d1 * im1), total_of(r1 * im1), total_of(im1 * im1)), fsnd, fgath, s_f, r_f)

    sol1 = sol[...] + alpha0 * dirn[...]
    def others(ref):
        return ref.at[pl.ds(1, 3)], ref.at[0, pl.ds(1, 3)], ref.at[0, 0, pl.ds(1, 3)]

    for w in (0, 1):
        for ref in others(bufs[w]):
            await_(ref, s_blk.at[w])
    for ref in others(igath):
        await_(ref, s_i.at[0])


    both = told(fgath, r_f)
    alpha1 = norm1 / take(both, 0)
    norm2 = norm1 + alpha1 * (alpha1 * take(both, 2) - 2.0 * take(both, 1))
    r2 = r1 - alpha1 * im1
    outs[0:8, :] = sol1 + alpha1 * d1
    outs[8:16, :] = r2
    outs[16:24, :] = r2 + (norm2 / norm1) * d1
    await_(fgath.at[pl.ds(1, 2 * CHIPS - 1)], s_f.at[0])


def per_device(points, inv_length, out_scale, noise, solution, residual, direction):
    vm = pl.BlockSpec(memory_space=pltpu.VMEM)
    hbm = pl.BlockSpec(memory_space=pl.ANY)
    sm = pl.BlockSpec(memory_space=pltpu.SMEM)
    V, D = pltpu.VMEM, pltpu.SemaphoreType.DMA
    out = pl.pallas_call(
        kernel,
        out_shape=jax.ShapeDtypeStruct((3 * VEC, COLS), f32),
        in_specs=[hbm, sm, sm, sm, hbm, hbm, hbm],
        out_specs=vm,
        scratch_shapes=[
            V((4, 4, 4, 40, HALF), f32), V((4, 4, 4, VEC, COLS), f32), V((4, 4, 4, VEC, COLS), f32),
            V((2 * CHIPS, 1, 128), f32), V((VEC, COLS), f32), V((1, 128), f32),
            V((8, 16, HALF), f32), V((2, 128, 2 * COLS), bf16),
            V((CHIPS, COLS, 2 * COLS), bf16), V((CHIPS, COLS, 2 * COLS), bf16),
            V((16, 2 * COLS), f32), V((16, 2 * COLS), f32), V((16, 2 * COLS), f32),
            V((24, HALF), f32), V((2, VEC, COLS), f32), V((2, VEC, COLS), f32),
            V((2, 1, 128), f32), V((2, 1, 128), f32),
            D((2,)), D((2, 8)), D((1,)), D((GROUPS,)), D((1,)), D((1,)), D((5,)), D((5,)),
            V((FEAT, COLS), f32), V((VEC, COLS), f32), V((VEC, COLS), f32), V((VEC, COLS), f32), D((4,)),
        ],
        compiler_params=pltpu.CompilerParams(
            collective_id=0, has_side_effects=True, vmem_limit_bytes=56 * 2**20
        ),
        name="cg",
    )(points, inv_length, out_scale, noise, solution, residual, direction)
    return out[0:8], out[8:16], out[16:24]


def solution(mesh):
    cols = P(None, ("grp", "mem"))
    return jax.shard_map(
        per_device,
        mesh=mesh,
        in_specs=(cols, P(), P(), P(), cols, cols, cols),
        out_specs=(cols, cols, cols),
        check_vma=False,
    )
```

```python
import math

import jax
import jax.numpy as jnp
from jax import lax
from jax.experimental import pallas as pl
from jax.experimental.pallas import tpu as pltpu
from jax.sharding import PartitionSpec as P

MESH = pl.DeviceIdType.MESH
f32 = jnp.float32
bf16 = jnp.bfloat16

FEAT = 11
VEC = 8
COLS = 256
HALF = 128
CHIPS = 64
GROUPS = 7
LOG2E = math.log2(math.e)
LIFT = 1.5 * LOG2E
SHIFT = 0.75 * LOG2E * LOG2E
SCALE = math.exp(1.5) / (3.0 * LOG2E * LOG2E)


def offsets():
    three = (2, 3, 1)
    out = [(i, j, k) for k in three for j in three for i in three]
    out += [(0, j, k) for k in three for j in three]
    out += [(i, 0, k) for k in three for i in three]
    out += [(i, j, 0) for j in three for i in three]
    out += [(0, 0, k) for k in three] + [(0, j, 0) for j in three] + [(i, 0, 0) for i in three]
    return out


OFFS = offsets()


def hops(off):
    return sum((0, 1, 2, 1)[d] for d in off)


PLANE = [(1, 1), (3, 3), (1, 3), (3, 1), (2, 1), (1, 2), (2, 3), (3, 2), (2, 2)]


def split3(rows):
    high = rows.astype(bf16)
    rest = rows - high.astype(f32)
    mid = rest.astype(bf16)
    low = (rest - mid.astype(f32)).astype(bf16)
    return high, mid, low


def col_stack(rows):
    h, m, l = split3(rows)
    one = jnp.ones((16, HALF), bf16)
    return jnp.concatenate([h, h, m, m, h, l, one, jnp.zeros_like(one)], 0)


def row_stack(rows, sq):
    h, m, l = split3(rows)
    row = lax.broadcasted_iota(jnp.int32, (16, HALF), 0)
    last = jnp.zeros((16, HALF), f32)
    for n, part in enumerate(split3(sq)):
        last = jnp.where(row == n, part.astype(f32), last)
    return jnp.concatenate([h, m, h, m, l, h, last.astype(bf16), jnp.zeros((16, HALF), bf16)], 0)


def vec_stack(rows):
    high = rows.astype(bf16).astype(f32)
    return jnp.concatenate([high, rows - high], 0).astype(bf16)


def tile_of(t):
    t = jnp.maximum(t, 1e-30)
    w = -LIFT - t * lax.rsqrt(t)
    return (w * w + SHIFT) * jnp.exp2(w)


def mv(x, k):
    return jnp.dot(x, k, preferred_element_type=f32)


def fold(acc):
    return acc[0:VEC] + acc[VEC : 2 * VEC]


def kernel(
    pts_in, inv, scale, noise, sol_in, res_in, dirn_in,
    outs,
    gath, rgath, igath, fgath, isnd, fsnd,
    qtmp, qmat, khi, klo, acc_d, acc_r, acc_i,
    ex_p, ex_s, ex_r, sc_s, sc_r,
    s_blk, r_blk, s_i, r_i, s_f, r_f, s_x, r_x,
    pts, sol, res, dirn, s_in,
):
    g, m = lax.axis_index("grp"), lax.axis_index("mem")
    x, y, z, core = g // 8, (g // 2) % 4, (m // 2) * 2 + g % 2, m % 2
    partner = (g, (m // 2) * 2 + 1 - core)

    at_x = [((x + e) % 4) * 8 for e in range(4)]
    at_y = [((y + e) % 4) * 2 for e in range(4)]
    at_z = [(z + e) % 4 for e in range(4)]
    odd_z = [v % 2 for v in at_z]
    high_z = [(v // 2) * 2 for v in at_z]
    both = [(i, j) for i in range(4) for j in range(4)]
    outer = {(i, j): jnp.where(core == 0, at_x[i] + odd_z[j], at_x[j] + odd_z[i]) for i, j in both}
    inner = {(i, j): jnp.where(core == 0, high_z[j], high_z[i]) for i, j in both}

    def peer(e1, e2, e3, other=0):
        return (outer[e1, e3] + at_y[e2], inner[e1, e3] + (1 - core if other else core))

    loads = (pts_in, pts), (dirn_in, dirn), (res_in, res), (sol_in, sol)
    loads = [pltpu.make_async_copy(a, b, s_in.at[n]) for n, (a, b) in enumerate(loads)]
    for cp in loads:
        cp.start()
    barrier = pltpu.get_barrier_semaphore()

    def greet(device):
        pl.semaphore_signal(barrier, inc=1, device_id=device, device_id_type=MESH)

    greet(partner)
    for e in (1, 3, 2):
        greet(peer(e, 0, 0))
        greet(peer(0, e, 0))
        greet(peer(0, 0, e))
    for e1, e2 in PLANE:
        greet(peer(e1, e2, 0))

    gain = math.sqrt(5.0) * LOG2E
    own, r_own = gath.at[0, 0, 0], rgath.at[0, 0, 0]
    for cp in loads[:2]:
        cp.wait()
    for half, (at, at_sq) in enumerate(((16, 27), (29, 28))):
        lanes = slice(half * HALF, (half + 1) * HALF)
        own[8 * half : 8 * half + 8, :] = dirn[:, lanes]
        sq = jnp.zeros((1, HALF), f32)
        for f in range(FEAT):
            scaled = pts[f : f + 1, lanes] * (inv[f] * gain)
            own[at + f : at + f + 1, :] = scaled
            sq = sq + scaled * scaled
        own[at_sq : at_sq + 1, :] = sq

    def put(src, dst, s, r, device):
        cp = pltpu.make_async_remote_copy(
            src_ref=src, dst_ref=dst, send_sem=s, recv_sem=r, device_id=device, device_id_type=MESH
        )
        cp.start()
        return cp

    def await_(ref, sem):
        pltpu.make_async_copy(ref, ref, sem).wait()

    def exchange(n, src, dst):
        return put(src, dst, s_x.at[n], r_x.at[n], partner)

    bufs = gath, rgath

    def send(w, src, dst, n, device):
        put(bufs[w].at[src], bufs[w].at[dst], s_blk.at[w], r_blk.at[w, n], device)

    def nine(w, n):
        await_(bufs[w].at[pl.ds(0, 3), pl.ds(0, 3), 0], r_blk.at[w, n])

    def leave(w):
        for e in (1, 3, 2):
            send(w, (0, 0, 0), (0, 0, e), 0, peer(e, 0, 0))
            send(w, (0, 0, 0), (0, e, 0), 0, peer(0, e, 0))
        for e in (1, 3, 2):
            send(w, (0, 0, 0), (e, 0, 0), 1, peer(0, 0, e))
        for e1, e2 in PLANE:
            send(w, (0, 0, 0), (0, e2, e1), 2, peer(e1, e2, 0))

    def pass_lines(w):
        await_(bufs[w].at[pl.ds(0, 2), pl.ds(0, 3), 0], r_blk.at[w, 0])
        for f in (1, 3, 2):
            send(w, (0, 0, pl.ds(1, 3)), (f, 0, pl.ds(1, 3)), 3, peer(0, 0, f))
        for f in (1, 3, 2):
            for e in (1, 3, 2):
                send(w, (0, e, 0), (f, e, 0), 4, peer(0, 0, f))
        await_(bufs[w].at[pl.ds(0, 3), 0, 0], r_blk.at[w, 1])

    def pass_plane(w):
        nine(w, 2)
        for f in (1, 3, 2):
            for e in (1, 3, 2):
                send(w, (0, e, pl.ds(1, 3)), (f, e, pl.ds(1, 3)), 4 + f, peer(0, 0, f))

    def rows_side(blk, top, start, n):
        pairs = [(half, cols) for half in (0, 1) for cols in (0, 1)]
        for half, cols in pairs:
            at = (16, 29)[half] - top
            put_at, one_at = ((0, 11), (5, 4))[cols]
            tmp = qtmp.at[n + 2 * half + cols]
            tmp[put_at : put_at + FEAT, :] = -2.0 * blk[at : at + FEAT, :]
            tmp[one_at : one_at + 1, :] = jnp.ones((1, HALF), f32)
        for half, cols in pairs:
            at_sq = (27, 28)[half] - top
            lanes = slice(start + half * HALF, start + (half + 1) * HALF)
            rows = qtmp[n + 2 * half + cols]
            qmat[cols, :, lanes] = row_stack(rows, blk[at_sq : at_sq + 1, :])

    pl.semaphore_wait(barrier, 19)
    cp_p = exchange(0, own.at[pl.ds(16, 24)], ex_p)
    leave(0)
    for acc in (acc_d, acc_r, acc_i, qtmp):
        acc[...] = jnp.zeros_like(acc)
    rows_side(own, 0, 0, 0)
    for cp in loads[2:]:
        cp.wait()
    r_own[...] = res[...]
    cp_p.wait()
    rows_side(ex_p, 16, COLS, 4)

    def build(places, starts=(0, 256)):
        for e3, e2, e1 in places:
            k = e3 * 16 + e2 * 4 + e1
            blk = gath.at[e3, e2, e1]
            cols = col_stack(blk[16:32, :]), col_stack(blk[24:40, :])
            vec = vec_stack(blk[0:8, :]), vec_stack(blk[8:16, :])
            for i0 in starts:
                part = acc_d[:, i0 : i0 + 256]
                for half in (0, 1):
                    j0 = half * HALF
                    t = lax.dot_general(
                        cols[half], qmat[half, :, i0 : i0 + 256],
                        (((0,), (0,)), ((), ())), preferred_element_type=f32,
                    )
                    tile = tile_of(t)
                    hi = tile.astype(bf16)
                    lo = (tile - hi.astype(f32)).astype(bf16)
                    khi[k, j0 : j0 + HALF, i0 : i0 + 256] = hi
                    klo[k, j0 : j0 + HALF, i0 : i0 + 256] = lo
                    part = part + mv(vec[half], hi) + mv(vec[half], lo)
                acc_d[:, i0 : i0 + 256] = part

    def times(acc, places, rows_of, starts=(0, 256)):
        for i0 in starts:
            part = acc[:, i0 : i0 + 256]
            for e3, e2, e1 in places:
                k = e3 * 16 + e2 * 4 + e1
                v = vec_stack(rows_of(e3, e2, e1))
                part = part + mv(v, khi[k, :, i0 : i0 + 256]) + mv(v, klo[k, :, i0 : i0 + 256])
            acc[:, i0 : i0 + 256] = part

    def pick(grp, *cases):
        out = cases[-1]
        for n in range(len(cases) - 2, -1, -1):
            out = jnp.where(grp == n, cases[n], out)
        return out

    def third(grp):
        return pick(grp, 0, 0, 0, 0, 1, 3, 2)

    def places_of(grp):
        e = third(grp)
        return [
            (
                pick(grp, p if q == 3 else 0, 0, q, q, e),
                pick(grp, p if q == 2 else 0, q, 0, p, q),
                pick(grp, p if q == 1 else 0, p, p, 0, p),
            )
            for q in range(1, 4)
            for p in range(1, 4)
        ]

    build([(0, 0, 0)])
    pass_lines(0)

    @pl.loop(0, GROUPS - 1)
    def _(grp):
        @pl.when(grp == 1)
        def _():
            pass_plane(0)

        @pl.when(grp == 2)
        def _():
            nine(0, 3)

        @pl.when(grp == 3)
        def _():
            nine(0, 4)
            leave(1)

        @pl.when(grp >= 4)
        def _():
            nine(0, 4 + third(grp))

        @pl.when(grp == 5)
        def _():
            pass_lines(1)

        build(places_of(grp))

    last = [(2, j, i) for j in range(1, 4) for i in range(1, 4)]
    nine(0, 6)
    pass_plane(1)
    build(last, (256,))
    ex_s[0] = fold(acc_d[:, COLS:])
    cp_a = exchange(1, ex_s.at[0], ex_r.at[0])
    build(last, (0,))
    total = fold(acc_d[:, :COLS])
    cp_a.wait()

    kd = (SCALE * scale[0]) * (total + ex_r[0])
    image = kd + noise[0] * dirn[...]
    isnd[...] = image
    igath[0, 0, 0] = image
    for n, (e1, e2, e3) in enumerate(OFFS):
        put(isnd, igath.at[e3, e2, e1], s_i.at[0], r_i.at[n // 9], peer(e1, e2, e3))

    lane = lax.broadcasted_iota(jnp.int32, (VEC, 128), 1)
    sub = lax.broadcasted_iota(jnp.int32, (VEC, 128), 0)

    def pack(*cols):
        out = jnp.zeros((VEC, 128), f32)
        for n, c in enumerate(cols):
            out = jnp.where(lane == n * VEC + sub, c, out)
        return jnp.sum(out, axis=0, keepdims=True)

    def take(a, n):
        return jnp.sum(jnp.where(lane == n * VEC + sub, a, 0.0), axis=1, keepdims=True)

    def total_of(a):
        return jnp.sum(a, axis=1, keepdims=True)

    def tell(row, src, dst, s, r):
        src[...] = row
        dst[0] = row
        every = [(e, other) for other in (0, 1) for e in OFFS + [(0, 0, 0)] * other]
        for (e1, e2, e3), other in sorted(every, key=lambda e: -hops(e[0])):
            k = other * CHIPS + e3 * 16 + e2 * 4 + e1
            put(src, dst.at[k], s.at[0], r.at[0], peer(e1, e2, e3, other))

    def told(dst, r):
        await_(dst.at[pl.ds(1, 2 * CHIPS - 1)], r.at[0])
        return jnp.sum(dst[...], axis=0)


    times(acc_r, [(0, 0, 0)], lambda e3, e2, e1: rgath[e3, e2, e1])
    nine(1, 3)

    @pl.loop(0, GROUPS)
    def _(grp):
        @pl.when(grp == 3)
        def _():
            nine(1, 4)

        @pl.when(grp >= 4)
        def _():
            nine(1, 4 + third(grp))

        times(acc_r, places_of(grp), lambda e3, e2, e1: rgath[e3, e2, e1])

    def image_of(e3, e2, e1):
        return igath[e3, e2, e1]

    def met(n):
        await_(igath.at[pl.ds(0, 3), pl.ds(0, 3), 0], r_i.at[n])

    times(acc_i, [(0, 0, 0)], image_of)

    def sums(acc, places):
        rr, di = acc
        for e3, e2, e1 in places:
            blk, r = gath.at[e3, e2, e1], rgath[e3, e2, e1]
            d = jnp.concatenate([blk[0:8, :], blk[8:16, :]], 1)
            rr = rr + r * r
            di = di + d * igath[e3, e2, e1]
        return rr, di

    def r1_sq(acc, places):
        for e3, e2, e1 in places:
            v = rgath[e3, e2, e1] - alpha0 * igath[e3, e2, e1]
            acc = acc + v * v
        return acc

    EARLY = 4

    @pl.loop(0, EARLY)
    def _(back):
        met(back)
        times(acc_i, places_of(GROUPS - 1 - back), image_of)

    late = [
        [(j, 0, i) for j in range(1, 4) for i in range(1, 4)],
        [(0, j, i) for j in range(1, 4) for i in range(1, 4)],
        [(k, 0, 0) for k in (2, 3, 1)] + [(0, j, 0) for j in (2, 3, 1)] + [(0, 0, i) for i in (2, 3, 1)],
    ]
    zero = jnp.zeros((VEC, COLS), f32)
    full = [(j, i) for j in range(4) for i in range(4)]
    deep = [(j, i) for j in range(1, 4) for i in range(4)]
    acc = lax.fori_loop(1, 4, lambda k, acc: sums(acc, [(k, j, i) for j, i in deep]), (zero, zero))
    acc = sums(acc, [(0, 0, 0)])
    for n, places in enumerate(late):
        met(EARLY + n)
        acc = sums(acc, places)
    mine = pack(total_of(acc[0]), total_of(acc[1]))
    sc_s[0] = mine
    cp_b = exchange(2, sc_s.at[0], sc_r.at[0])
    times(acc_i, late[0] + late[1], image_of)
    cp_b.wait()
    both = mine + sc_r[0]
    norm0 = take(both, 0)
    alpha0 = norm0 / take(both, 1)
    acc = lax.fori_loop(0, 4, lambda k, acc: r1_sq(acc, [(k, j, i) for j, i in full]), zero)
    mine = pack(total_of(acc))
    sc_s[1] = mine
    cp_c = exchange(3, sc_s.at[1], sc_r.at[1])
    times(acc_i, late[2], image_of, (256,))
    ex_s[1] = fold(acc_r[:, COLS:]) - alpha0 * fold(acc_i[:, COLS:])
    cp_d = exchange(4, ex_s.at[1], ex_r.at[1])
    times(acc_i, late[2], image_of, (0,))
    part = fold(acc_r[:, :COLS]) - alpha0 * fold(acc_i[:, :COLS])
    r1 = res[...] - alpha0 * image
    cp_c.wait()
    norm1 = take(mine + sc_r[1], 0)
    beta = norm1 / norm0
    d1 = r1 + beta * dirn[...]
    cp_d.wait()
    im1 = (SCALE * scale[0]) * (part + ex_r[1]) + beta * kd + noise[0] * d1
    tell(pack(total_of(d1 * im1), total_of(r1 * im1), total_of(im1 * im1)), fsnd, fgath, s_f, r_f)

    sol1 = sol[...] + alpha0 * dirn[...]
    def others(ref):
        return ref.at[pl.ds(1, 3)], ref.at[0, pl.ds(1, 3)], ref.at[0, 0, pl.ds(1, 3)]

    for w in (0, 1):
        for ref in others(bufs[w]):
            await_(ref, s_blk.at[w])
    for ref in others(igath):
        await_(ref, s_i.at[0])


    both = told(fgath, r_f)
    alpha1 = norm1 / take(both, 0)
    norm2 = norm1 + alpha1 * (alpha1 * take(both, 2) - 2.0 * take(both, 1))
    r2 = r1 - alpha1 * im1
    outs[0:8, :] = sol1 + alpha1 * d1
    outs[8:16, :] = r2
    outs[16:24, :] = r2 + (norm2 / norm1) * d1
    await_(fgath.at[pl.ds(1, 2 * CHIPS - 1)], s_f.at[0])


def per_device(points, inv_length, out_scale, noise, solution, residual, direction):
    vm = pl.BlockSpec(memory_space=pltpu.VMEM)
    hbm = pl.BlockSpec(memory_space=pl.ANY)
    sm = pl.BlockSpec(memory_space=pltpu.SMEM)
    V, D = pltpu.VMEM, pltpu.SemaphoreType.DMA
    out = pl.pallas_call(
        kernel,
        out_shape=jax.ShapeDtypeStruct((3 * VEC, COLS), f32),
        in_specs=[hbm, sm, sm, sm, hbm, hbm, hbm],
        out_specs=vm,
        scratch_shapes=[
            V((4, 4, 4, 40, HALF), f32), V((4, 4, 4, VEC, COLS), f32), V((4, 4, 4, VEC, COLS), f32),
            V((2 * CHIPS, 1, 128), f32), V((VEC, COLS), f32), V((1, 128), f32),
            V((8, 16, HALF), f32), V((2, 128, 2 * COLS), bf16),
            V((CHIPS, COLS, 2 * COLS), bf16), V((CHIPS, COLS, 2 * COLS), bf16),
            V((16, 2 * COLS), f32), V((16, 2 * COLS), f32), V((16, 2 * COLS), f32),
            V((24, HALF), f32), V((2, VEC, COLS), f32), V((2, VEC, COLS), f32),
            V((2, 1, 128), f32), V((2, 1, 128), f32),
            D((2,)), D((2, 8)), D((1,)), D((GROUPS,)), D((1,)), D((1,)), D((5,)), D((5,)),
            V((FEAT, COLS), f32), V((VEC, COLS), f32), V((VEC, COLS), f32), V((VEC, COLS), f32), D((4,)),
        ],
        compiler_params=pltpu.CompilerParams(
            collective_id=0, has_side_effects=True, vmem_limit_bytes=56 * 2**20
        ),
        name="cg",
    )(points, inv_length, out_scale, noise, solution, residual, direction)
    return out[0:8], out[8:16], out[16:24]


def solution(mesh):
    cols = P(None, ("grp", "mem"))
    return jax.shard_map(
        per_device,
        mesh=mesh,
        in_specs=(cols, P(), P(), P(), cols, cols, cols),
        out_specs=(cols, cols, cols),
        check_vma=False,
    )
```
